128 devices in a mesh: gx: 16 (over x, y_hi, core), gy: 8 (over z, y_lo).
Axes of the slice: x: 4, y: 4 (y_hi: 2, y_lo: 2; y = y_hi * 2 + y_lo), z: 4, core: 2. Of those that a mesh axis runs over, the one named last changes fastest.
Arguments:
- fields: float32 [14, 48, 256, 1024], P(None, None, 'gx', 'gy'), may hold values from -1.5 to 9, as said below
- register: float32 [14, 48, 256, 1024], P(None, None, 'gx', 'gy'), may hold values from -0.15 to 0.15
Outputs:
- fields_next: float32 [14, 48, 256, 1024], P(None, None, 'gx', 'gy')
- register_next: float32 [14, 48, 256, 1024], P(None, None, 'gx', 'gy')
- flame_metrics: bfloat16 [5, 48, 256, 1024], P(None, 'gy', 'gx')
The draws below stay inside these ranges and needn't reach their ends.
Inputs may be any that keep to these rules, and one draw needn't show every extreme that they name: fields[0] lies in 0.5 to 1.5; velocities fields[1:4] / fields[0] lie within -1 to 1; fields[4] / fields[0] minus half the squared speed lies in 1 to 4; each species density over fields[0] lies in 0.01 to 0.7.
All inputs are finite; a program needn't handle non-finite values.
Results may differ from the reference program's by a relative error of at most 0.0014.
The reference program's roundings to bfloat16 on the way (of `probe`) count: a program that leaves them out, or rounds other values in their place, can miss the bound.
Values may be sent and summed in bfloat16 or wider, within the bound.
A program may use at most 192 MiB of HBM per device.

```python
import math
import jax
import jax.numpy as jnp
import numpy as np
from jax import lax

FIELDS = 14
CX = 16
CY = 128
Z = 48
NX = 256
NY = 1024


def wave_stack(key, count, weights):
    phases = jax.random.uniform(key, (3, count, 1, 1, 1), jnp.float32, 0.0, 2.0 * math.pi)
    turns_first = max(NX // (2 * CX), 1)
    turns_second = max(NY // (2 * CY), 1)
    depth = jnp.arange(Z, dtype=jnp.float32).reshape(1, Z, 1, 1)
    across = jnp.arange(NX, dtype=jnp.float32).reshape(1, 1, NX, 1)
    lengthwise = jnp.arange(NY, dtype=jnp.float32).reshape(1, 1, 1, NY)
    first = jnp.sin(across * (2.0 * math.pi * turns_first / NX) + phases[0])
    second = jnp.sin(lengthwise * (2.0 * math.pi * turns_second / NY) + phases[1])
    third = jnp.sin(depth * (2.0 * math.pi / Z) + phases[2])
    return weights[0] * first + weights[1] * second + weights[2] * third


def draw_fields(key, part):
    key = jax.random.fold_in(key, 7)
    keys = jax.random.split(key, 11)
    grid = (Z, NX, NY)
    weights = (0.5, 0.3, 0.2)
    density_noise = jax.random.uniform(keys[1], (1,) + grid, jnp.float32, -1.0, 1.0)
    speed_noise = jax.random.uniform(keys[4], (3,) + grid, jnp.float32, -1.0, 1.0)
    heat_noise = jax.random.uniform(keys[7], (1,) + grid, jnp.float32, -1.0, 1.0)
    species_noise = jax.random.uniform(keys[10], (9,) + grid, jnp.float32, -1.0, 1.0)
    density = (1.0 + 0.2 * wave_stack(keys[0], 1, weights) + 0.02 * density_noise)[0]
    means = jnp.asarray([0.6, 0.45, 0.0], jnp.float32).reshape(3, 1, 1, 1)
    velocity = means + 0.3 * wave_stack(keys[3], 3, weights) + 0.03 * speed_noise
    internal = (1.7 + 0.5 * wave_stack(keys[6], 1, weights) + 0.04 * heat_noise)[0]
    center = jnp.asarray([0.045, 0.08, 0.016, 0.016, 0.2, 0.0125, 0.016, 0.016, 0.55], jnp.float32).reshape(9, 1, 1, 1)
    amplitude = jnp.asarray([0.015, 0.02, 0.004, 0.004, 0.1, 0.0015, 0.004, 0.004, 0.1], jnp.float32).reshape(9, 1, 1, 1)
    width = jnp.asarray([0.005, 0.005, 0.001, 0.001, 0.05, 0.0005, 0.001, 0.001, 0.03], jnp.float32).reshape(9, 1, 1, 1)
    fractions = center + amplitude * wave_stack(keys[9], 9, weights) + width * species_noise
    kinetic = 0.5 * (velocity[0] * velocity[0] + velocity[1] * velocity[1] + velocity[2] * velocity[2])
    energy = density * (internal + kinetic)
    species = density * fractions
    return jnp.concatenate([density[None], density * velocity, energy[None], species], axis=0).astype(jnp.float32)


def block_levels(stream_key, shape, shards, smallest, largest):
    level, own = 1.0, jax.random.fold_in(stream_key, 6)
    for axis_at, blocks in shards:
        steps = jnp.exp(jax.random.uniform(jax.random.fold_in(own, axis_at), (blocks,), jnp.float32, smallest / len(shards), largest / len(shards)))
        level = level * jnp.repeat(steps, shape[axis_at] // blocks).reshape([-1 if axis == axis_at else 1 for axis in range(len(shape))])
    return level


def setup_inputs(seed: int = 0) -> dict:
    splits = jax.random.split(jax.random.key(seed), 3)
    fields = draw_fields(jax.random.fold_in(splits[2], 71), 0)
    register = jnp.clip(jax.random.uniform(splits[1], (FIELDS, Z, NX, NY), jnp.float32, -0.15, 0.15) * block_levels(splits[1], (FIELDS, Z, NX, NY), ((2, 16), (3, 8)), -0.4, 0.0), -0.15, 0.15)
    return dict(fields=fields, register=register)


GAMMA_LESS = 0.4
UNIVERSAL_R = 0.25
TIME_STEP = 0.25
SECTION_DECAY = -0.4178904745
SECTION_WEIGHT = 0.3792103129
GRAD_FLOOR = 0.1
PROGRESS_SCALE = 4.0
CENTRAL_WEIGHTS = (0.8, -0.2, 4.0 / 105.0, -1.0 / 280.0)
MOLAR_MASS = (2.0, 32.0, 16.0, 17.0, 18.0, 1.0, 33.0, 34.0, 28.0)
FORMATION_HEAT = (0.0, 0.0, 2.0, 0.3, -1.5, 3.0, 0.1, -0.4, 0.0)
ARRHENIUS_LIST = ((5, 1, (2, 3), 40.0, 2.0), (2, 0, (5, 3), 30.0, 1.2), (3, 0, (5, 4), 25.0, 0.8), (2, 4, (3, 3), 10.0, 1.6), (5, 1, (6,), 15.0, 0.2), (6, 5, (3, 3), 20.0, 0.3), (6, 6, (7, 1), 12.0, 0.4), (7, 8, (3, 3, 8), 8.0, 1.8))

def make_table():
    table = np.zeros((14, 8))
    for column, kinetic_step_record in enumerate(ARRHENIUS_LIST):
        change = np.zeros(9)
        change[kinetic_step_record[0]] -= 1.0
        change[kinetic_step_record[1]] -= 1.0
        for product in kinetic_step_record[2]:
            change[product] += 1.0
        for species in range(9):
            mass_change = MOLAR_MASS[species] / 18.0 * change[species]
            table[5 + species, column] = mass_change
            table[4, column] -= FORMATION_HEAT[species] * mass_change
    return table

def inverse_weights():
    return np.array([18.0 / value for value in MOLAR_MASS])

def primitives(fields):
    velocity = fields[1:4] / fields[0]
    static_stress = GAMMA_LESS * (fields[4] - 0.5 * (fields[1] * velocity[0] + fields[2] * velocity[1] + fields[3] * velocity[2]))
    return (velocity, static_stress)

def reaction_rates(fields, static_stress):
    species_quantities = fields[5:14] * jnp.asarray(inverse_weights(), jnp.float32).reshape(9, 1, 1, 1)
    summed_quantity = lax.optimization_barrier(jnp.sum(species_quantities, axis=0))
    cell_thermal_state = static_stress / (UNIVERSAL_R * summed_quantity)
    return jnp.stack([kinetic_step_record[3] * jnp.exp(-kinetic_step_record[4] / cell_thermal_state) * species_quantities[kinetic_step_record[0]] * species_quantities[kinetic_step_record[1]] for kinetic_step_record in ARRHENIUS_LIST])

def rolled_central(values, along):
    total = jnp.zeros_like(values)
    for offset, weight in enumerate(CENTRAL_WEIGHTS, 1):
        total = total + weight * (jnp.roll(values, -offset, along) - jnp.roll(values, offset, along))
    return total

def flame_metrics(padded):
    scalar = padded[0]
    grad_z = (scalar[2:, 1:-1, 1:-1] - scalar[:-2, 1:-1, 1:-1]) * 0.5
    grad_x = (scalar[1:-1, 2:, 1:-1] - scalar[1:-1, :-2, 1:-1]) * 0.5
    grad_y = (scalar[1:-1, 1:-1, 2:] - scalar[1:-1, 1:-1, :-2]) * 0.5
    magnitude = jnp.maximum(jnp.sqrt(grad_x * grad_x + grad_y * grad_y + grad_z * grad_z), GRAD_FLOOR)
    normal_x = -grad_x / magnitude
    normal_y = -grad_y / magnitude
    normal_z = -grad_z / magnitude
    curvature = 0.5 * (normal_x[1:-1, 2:, 1:-1] - normal_x[1:-1, :-2, 1:-1])
    curvature = curvature + 0.5 * (normal_y[1:-1, 1:-1, 2:] - normal_y[1:-1, 1:-1, :-2])
    curvature = curvature + 0.5 * (normal_z[2:, 1:-1, 1:-1] - normal_z[:-2, 1:-1, 1:-1])
    inner = (normal_x[1:-1, 1:-1, 1:-1], normal_y[1:-1, 1:-1, 1:-1], normal_z[1:-1, 1:-1, 1:-1])
    speeds = padded[1:4]
    gradients = []
    for component in range(3):
        piece = speeds[component]
        along_x = (piece[2:-2, 3:-1, 2:-2] - piece[2:-2, 1:-3, 2:-2]) * 0.5
        along_y = (piece[2:-2, 2:-2, 3:-1] - piece[2:-2, 2:-2, 1:-3]) * 0.5
        along_z = (piece[3:-1, 2:-2, 2:-2] - piece[1:-3, 2:-2, 2:-2]) * 0.5
        gradients.append((along_x, along_y, along_z))
    strain = gradients[0][0] + gradients[1][1] + gradients[2][2]
    for component in range(3):
        for direction in range(3):
            strain = strain - inner[component] * inner[direction] * gradients[component][direction]
    return jnp.stack([inner[0], inner[1], inner[2], curvature, strain])

def reference(fields, register):
    velocity, static_stress = primitives(fields)
    rates = reaction_rates(fields, static_stress)
    chem = jnp.asarray(make_table(), jnp.float32)

    def per_field(item):
        index, values, stored = item
        source = jnp.tensordot(chem[index], rates, axes=1, precision=lax.Precision.HIGHEST)
        advection = jnp.zeros_like(values)
        for direction, along in ((0, 1), (1, 2), (2, 0)):
            is_moment = (index == 1 + direction).astype(jnp.float32)
            is_energy = (index == 4).astype(jnp.float32)
            flux = values * velocity[direction] + static_stress * is_moment + static_stress * velocity[direction] * is_energy
            advection = advection + rolled_central(flux, along)
        stored_next = SECTION_DECAY * stored + TIME_STEP * (source - advection)
        return (values + SECTION_WEIGHT * stored_next, stored_next)
    indices = jnp.arange(fields.shape[0], dtype=jnp.int32)
    fields_next, register_next = lax.map(per_field, (indices, fields, register))
    probe = jnp.stack([PROGRESS_SCALE * (fields[9] / fields[0]), velocity[0], velocity[1], velocity[2]]).astype(jnp.bfloat16)
    padded = jnp.pad(probe.astype(jnp.float32), ((0, 0), (2, 2), (2, 2), (2, 2)), mode='wrap')
    metrics = flame_metrics(padded).astype(jnp.bfloat16)
    return (fields_next, register_next, metrics)
```

```python
import jax
import jax.numpy as jnp
import numpy as np
from jax import lax
from jax.experimental import pallas as pl
from jax.experimental.pallas import tpu as pltpu
from jax.sharding import PartitionSpec as P

MESH = pl.DeviceIdType.MESH
F32, BF16 = jnp.float32, jnp.bfloat16
DECAY = -0.4178904745
STEP = 0.25
WEIGHT = 0.3792103129
C = (0.8, -0.2, 4.0 / 105.0, -1.0 / 280.0)
MOLAR_MASS = (2.0, 32.0, 16.0, 17.0, 18.0, 1.0, 33.0, 34.0, 28.0)
FORMATION_HEAT = (0.0, 0.0, 2.0, 0.3, -1.5, 3.0, 0.1, -0.4, 0.0)
REACTIONS = (
    (5, 1, (2, 3), 40.0, 2.0),
    (2, 0, (5, 3), 30.0, 1.2),
    (3, 0, (5, 4), 25.0, 0.8),
    (2, 4, (3, 3), 10.0, 1.6),
    (5, 1, (6,), 15.0, 0.2),
    (6, 5, (3, 3), 20.0, 0.3),
    (6, 6, (7, 1), 12.0, 0.4),
    (7, 8, (3, 3, 8), 8.0, 1.8),
)
NF, NZ, CX, LY = 14, 48, 16, 128
ROWS = NZ * CX
HALF = ROWS // 2


def make_table():
    table = np.zeros((14, 8))
    for column, record in enumerate(REACTIONS):
        change = np.zeros(9)
        change[record[0]] -= 1.0
        change[record[1]] -= 1.0
        for product in record[2]:
            change[product] += 1.0
        for species in range(9):
            mass_change = MOLAR_MASS[species] / 18.0 * change[species]
            table[5 + species, column] = mass_change
            table[4, column] -= FORMATION_HEAT[species] * mass_change
    return table


TABLE = make_table()


def lane_weights():
    whole = (672.0, -168.0, 32.0, -3.0)
    inner = np.zeros((LY, LY))
    for out in range(LY):
        for m in range(1, 5):
            if out + m < LY:
                inner[out + m, out] += whole[m - 1]
            if out - m >= 0:
                inner[out - m, out] -= whole[m - 1]
    edge = np.zeros((2 * NF, 2 * LY, LY))
    for field in range(NF):
        for half in range(2):
            base = 8 * field + 4 * half
            for near in range(1, 5):
                for cell in range(1, 6 - near):
                    weight = whole[near + cell - 2]
                    edge[2 * field + half, base + 4 - near, cell - 1] = -weight
                    edge[2 * field + half, LY + base + near - 1, LY - cell] = weight
    return np.concatenate([inner, inner]).astype(jnp.bfloat16), edge.astype(jnp.bfloat16)


def rounded(x):
    return x.astype(BF16).astype(F32)


def shaped(h):
    q1 = rounded(h[0])
    e1 = q1 - h[0]
    q2 = rounded(h[1] + 4.0 * e1)
    left = C[0] * e1 + C[1] * (q2 - h[1])
    q3 = rounded(h[2] - left * (1.0 / C[2]))
    left = left + C[2] * (q3 - h[2])
    return q1, q2, q3, h[3] - left * (1.0 / C[3])


def shaped_lanes(x, layer, turn):
    roll = lambda a, n: pltpu.roll(a, (turn * n) % LY, 1)
    q1 = rounded(x)
    e1 = jnp.where(layer == 0, q1 - x, 0.0)
    q2 = rounded(x + 4.0 * roll(e1, 1))
    e2 = jnp.where(layer == 1, q2 - x, 0.0)
    left = C[0] * roll(e1, 1) + C[1] * e2
    left = roll(left, 1)
    q3 = rounded(x - left * (1.0 / C[2]))
    left = roll(jnp.where(layer == 2, left + C[2] * (q3 - x), 0.0), 1)
    q4 = rounded(x - left * (1.0 / C[3]))
    return jnp.where(layer == 0, q1, jnp.where(layer == 1, q2, jnp.where(layer == 2, q3, q4)))


def kernel(
    f_hbm, r_hbm, wd, wu, fo, ro, mo,
    VEL, PR, PX, TX, YH, NS, NZS, CV, M,
    xps, xpr, dgs, dgr, ys, yr, xs, xr,
    load_sem, xp_ss, xp_rs, dg_ss, dg_rs, y_ss, y_rs, x_ss, x_rs, m_ss, m_rs, own_sem,
):
    gx, gy = lax.axis_index("gx"), lax.axis_index("gy")
    nx, ny = lax.axis_size("gx"), lax.axis_size("gy")
    gxs = (lax.rem(gx + nx - 1, nx), lax.rem(gx + 1, nx))
    gys = (lax.rem(gy + ny - 1, ny), lax.rem(gy + 1, ny))

    barrier = pltpu.get_barrier_semaphore()
    partners = [(gxs[0], gy), (gxs[1], gy)]
    partners += [(gxs[a], gys[b]) for a in range(2) for b in range(2)]
    partners += [(gx, lax.rem(gy + d, ny)) for d in range(1, ny)]
    for partner in partners:
        pl.semaphore_signal(barrier, 1, device_id=partner, device_id_type=MESH)

    parts = [(f_hbm, fo, 0, 5), (f_hbm, fo, 9, 1), (f_hbm, fo, 5, 4), (f_hbm, fo, 10, 4), (r_hbm, ro, 0, 14)]
    loads = [
        pltpu.make_async_copy(a.at[pl.ds(s, n)], b.at[pl.ds(s, n)], load_sem.at[i])
        for i, (a, b, s, n) in enumerate(parts)
    ]
    for load in loads:
        load.start()
    loads[0].wait()
    loads[1].wait()

    def primitive(z, carry):
        rows = pl.ds(pl.multiple_of(z * CX, CX), CX)
        mine = pl.ds(pl.multiple_of(z * 32 + 8, 8), CX)
        inverse = 1.0 / fo[0, rows]
        moment = [fo[1 + d, rows] for d in range(3)]
        speed = [m * inverse for m in moment]
        PR[rows] = 0.4 * (fo[4, rows] - 0.5 * (moment[0] * speed[0] + moment[1] * speed[1] + moment[2] * speed[2]))
        PX[0, mine] = rounded(4.0 * (fo[9, rows] * inverse))
        for d in range(3):
            VEL[d, rows] = speed[d]
            PX[1 + d, mine] = rounded(speed[d])
        return carry

    lax.fori_loop(0, NZ, primitive, 0)

    lane48 = lax.broadcasted_iota(jnp.int32, (NZ, LY), 1)
    eye48 = lane48 == lax.broadcasted_iota(jnp.int32, (NZ, LY), 0)
    for side, (near, far) in enumerate(((0, 1), (15, 14))):
        xps[side, 0] = PX[0, pl.ds(8 + near, NZ, stride=32)].astype(BF16)
        xps[side, 1] = PX[0, pl.ds(8 + far, NZ, stride=32)].astype(BF16)
        for d in range(3):
            xps[side, 2 + d] = PX[1 + d, pl.ds(8 + near, NZ, stride=32)].astype(BF16)
        edge = PX[0, pl.ds(8 + near, NZ, stride=32)]
        for along, lane in enumerate((0, LY - 1)):
            column = jnp.sum(jnp.where(lane48 == lane, edge, 0.0), axis=1, keepdims=True)
            line = jnp.sum(jnp.where(eye48, column, 0.0), axis=0, keepdims=True)
            dgs[2 * side + along] = jnp.broadcast_to(line, (16, LY)).astype(BF16)

    pl.semaphore_wait(barrier, len(partners))

    def remote(src, dst, ss, rs, device):
        return pltpu.make_async_remote_copy(
            src_ref=src, dst_ref=dst, send_sem=ss, recv_sem=rs, device_id=device, device_id_type=MESH
        )

    xp_copy = [remote(xps.at[s], xpr.at[s], xp_ss.at[s], xp_rs.at[s], (gxs[s], gy)) for s in range(2)]
    dg_copy = [
        remote(dgs.at[n], dgr.at[n], dg_ss.at[n], dg_rs.at[n], (gxs[n // 2], gys[n % 2])) for n in range(4)
    ]
    for copy in xp_copy + dg_copy:
        copy.start()
    loads[2].wait()
    loads[3].wait()

    lane = lax.broadcasted_iota(jnp.int32, (CX, LY), 1)
    place = lane & 7
    layer = lane & 3

    def pack_y(i, carry):
        packed = []
        for half in range(2):
            rows = pl.ds(pl.multiple_of(half * HALF + i * CX, CX), CX)
            mine = pl.ds(pl.multiple_of((half * (NZ // 2) + i) * 32 + 8, 8), CX)
            v, p = VEL[1, rows], PR[rows]
            total = jnp.zeros((CX, LY), F32)
            for slot in range(16):
                if slot < NF:
                    flux = fo[slot, rows]
                    flux = (flux + p) * v if slot == 4 else flux * v
                    flux = flux + p if slot == 2 else flux
                elif slot == 14:
                    pu, pv = PX[1, mine], PX[2, mine]
                    flux = jnp.where(lane == 124, pltpu.roll(pu, 125, 1), PX[0, mine])
                    flux = jnp.where(lane == 125, pltpu.roll(pv, 126, 1), flux)
                    flux = jnp.where(lane == 2, pltpu.roll(pu, 2, 1), flux)
                    flux = jnp.where(lane == 3, pltpu.roll(pv, 3, 1), flux)
                else:
                    flux = PX[3, mine]
                total = jnp.where((lane >> 3) == slot, pltpu.roll(flux, (4 + 8 * slot) % LY, 1), total)
            packed.append(total)
        up = jnp.where(place < 4, packed[0], pltpu.roll(packed[1], 4, 1))
        low = jnp.where(place < 4, pltpu.roll(packed[0], LY - 4, 1), packed[1])
        rows = pl.ds(pl.multiple_of(i * CX, CX), CX)
        ys[0, rows] = shaped_lanes(low, layer, 1).astype(BF16)
        ys[1, rows] = shaped_lanes(up, 3 - layer, -1).astype(BF16)
        return carry

    lax.fori_loop(0, NZ // 2, pack_y, 0)
    y_copy = [remote(ys.at[s], yr.at[s], y_ss.at[s], y_rs.at[s], (gx, gys[s])) for s in range(2)]
    for copy in y_copy:
        copy.start()

    def x_copy(side, block):
        return remote(
            xs.at[side, block], xr.at[side, block], x_ss.at[side, block], x_rs.at[side, block], (gxs[side], gy)
        )

    def pack_x(block, carry):
        for side in range(2):
            at = [pl.ds(block * 256 + (n if side == 0 else 15 - n), 16, stride=CX) for n in range(4)]
            u = [VEL[0, a] for a in at]
            for k in range(NF):
                h = []
                for n in range(4):
                    flux = fo[k, at[n]]
                    flux = (flux + PR[at[n]]) * u[n] if k == 4 else flux * u[n]
                    h.append(flux + PR[at[n]] if k == 1 else flux)
                for n, q in enumerate(shaped(h)):
                    xs[side, block, pl.ds((4 * k + n) * 16, 16)] = q.astype(BF16)
            x_copy(side, block).start()
        return carry

    lax.fori_loop(0, 3, pack_x, 0)

    loads[4].wait()

    def chemistry(z, carry):
        rows = pl.ds(pl.multiple_of(z * CX, CX), CX)
        moles = [fo[5 + k, rows] * (18.0 / MOLAR_MASS[k]) for k in range(9)]
        total = moles[0]
        for k in range(1, 9):
            total = total + moles[k]
        cold = (0.25 * total) / PR[rows]
        rates = [
            record[3] * jnp.exp(-record[4] * cold) * (moles[record[0]] * moles[record[1]]) for record in REACTIONS
        ]
        for k in range(NF):
            result = DECAY * ro[k, rows]
            for r in range(8):
                if TABLE[k, r] != 0.0:
                    result = result + float(STEP * TABLE[k, r]) * rates[r]
            ro[k, rows] = result
        return carry

    lax.fori_loop(0, NZ, chemistry, 0)

    for s in range(2):
        xp_copy[s].wait_recv()
    for side, near, far in ((1, 7, 6), (0, 24, 25)):
        PX[0, pl.ds(near, NZ, stride=32)] = xpr[side, 0].astype(F32)
        PX[0, pl.ds(far, NZ, stride=32)] = xpr[side, 1].astype(F32)
        for d in range(3):
            PX[1 + d, pl.ds(near, NZ, stride=32)] = xpr[side, 2 + d].astype(F32)
    for n in range(4):
        dg_copy[n].wait_recv()
    for side, row in ((1, 7), (0, 24)):
        corner = []
        for along in (1, 0):
            line = dgr[2 * side + along].astype(F32)[0:1]
            corner.append(jnp.sum(jnp.where(eye48, line, 0.0), axis=1, keepdims=True))
        TX[pl.ds(row, NZ, stride=32)] = jnp.where(lane48 < 64, corner[0], corner[1])
    for s in range(2):
        y_copy[s].wait_recv()

    def turned(i, carry):
        for half in range(2):
            z = half * (NZ // 2) + i
            rows = pl.ds(pl.multiple_of(z * CX, CX), CX)
            mine = pl.ds(pl.multiple_of(z * 32 + 8, 8), CX)
            there = pl.ds(pl.multiple_of(i * CX, CX), CX)
            low, high = yr[1, there].astype(F32), yr[0, there].astype(F32)
            base = 112 + 4 * half
            put = lambda a, source, target: pltpu.roll(a, (target - source) % LY, 1)
            s = PX[0, mine]
            t = jnp.where(lane < 64, pltpu.roll(s, 2, 1), pltpu.roll(s, LY - 2, 1))
            t = jnp.where(lane < 2, put(low, base + 2, 0), t)
            TX[mine] = jnp.where(lane >= 126, put(high, base, 126), t)
            YH[0, rows] = jnp.where(lane < 64, put(low, base, 0), put(high, base + 2, 127))
            YH[1, rows] = jnp.where(lane < 64, put(low, base + 1, 0), put(high, base + 3, 127))
            YH[2, rows] = jnp.where(lane < 64, put(low, base + 11, 0), put(high, base + 8, 127))
        return carry

    lax.fori_loop(0, NZ // 2, turned, 0)

    def normals(z, carry):
        above, below = lax.rem(z + 1, NZ), lax.rem(z + NZ - 1, NZ)
        rows = pl.ds(pl.multiple_of(z * CX, CX), CX)

        def wide(ref, plane, shift):
            return ref[0, pl.ds(plane * 32 + 4 + shift, 24)]

        def mine(plane, shift=0):
            return pl.ds(plane * 32 + 8 + shift, CX)

        lane24 = lax.broadcasted_iota(jnp.int32, (24, LY), 1)
        s, t = wide(PX, z, 0), TX[pl.ds(z * 32 + 4, 24)]
        behind = jnp.where(lane24 == 0, pltpu.roll(t, LY - 1, 1), pltpu.roll(s, 1, 1))
        ahead = jnp.where(lane24 == LY - 1, pltpu.roll(t, 1, 1), pltpu.roll(s, LY - 1, 1))
        grad_x = 0.5 * (wide(PX, z, 1) - wide(PX, z, -1))
        grad_y = 0.5 * (ahead - behind)
        grad_z = 0.5 * (wide(PX, above, 0) - wide(PX, below, 0))
        scale = -lax.rsqrt(jnp.maximum(grad_x * grad_x + grad_y * grad_y + grad_z * grad_z, 0.01))
        NS[0], NS[1], NS[2] = grad_x * scale, grad_y * scale, grad_z * scale
        normal = [NS[d, 4:20] for d in range(3)]

        t = TX[mine(z)]
        edge_x = 0.5 * (TX[mine(z, 1)] - TX[mine(z, -1)])
        edge_y = 0.5 * (pltpu.roll(t, LY - 1, 1) - pltpu.roll(t, 1, 1))
        edge_z = 0.5 * (TX[mine(above)] - TX[mine(below)])
        edge = -edge_y * lax.rsqrt(jnp.maximum(edge_x * edge_x + edge_y * edge_y + edge_z * edge_z, 0.01))
        behind = jnp.where(lane == 0, pltpu.roll(edge, LY - 1, 1), pltpu.roll(normal[1], 1, 1))
        ahead = jnp.where(lane == LY - 1, pltpu.roll(edge, 1, 1), pltpu.roll(normal[1], LY - 1, 1))
        CV[rows] = 0.5 * (NS[0, 5:21] - NS[0, 3:19]) + 0.5 * (ahead - behind)
        NZS[rows] = normal[2]

        strain = None
        for d in range(3):
            speed, halo = PX[1 + d, mine(z)], YH[d, rows]
            behind = jnp.where(lane == 0, halo, pltpu.roll(speed, 1, 1))
            ahead = jnp.where(lane == LY - 1, halo, pltpu.roll(speed, LY - 1, 1))
            along = (
                0.5 * (PX[1 + d, mine(z, 1)] - PX[1 + d, mine(z, -1)]),
                0.5 * (ahead - behind),
                0.5 * (PX[1 + d, mine(above)] - PX[1 + d, mine(below)]),
            )
            inner = normal[0] * along[0] + normal[1] * along[1] + normal[2] * along[2]
            term = along[d] - normal[d] * inner
            strain = term if strain is None else strain + term
        for d in range(3):
            M[d, z] = normal[d].astype(BF16)
        M[4, z] = strain.astype(BF16)
        return carry

    lax.fori_loop(0, NZ, normals, 0)

    depth = NZ // 8

    def curve(z, carry):
        above, below = lax.rem(z + 1, NZ), lax.rem(z + NZ - 1, NZ)
        at = lambda plane: pl.ds(pl.multiple_of(plane * CX, CX), CX)
        M[3, z] = (CV[at(z)] + 0.5 * (NZS[at(above)] - NZS[at(below)])).astype(BF16)
        return carry

    lax.fori_loop(0, NZ, curve, 0)
    land = mo.at[:, :, :, pl.ds(pl.multiple_of(gy * LY, LY), LY)]

    def m_copy(d):
        target = lax.rem(gy + d, ny)
        return remote(M.at[:, pl.ds(target * depth, depth)], land, m_ss.at[d], m_rs.at[d], (gx, target))

    for d in range(1, 8):
        m_copy(d).start()
    own = pltpu.make_async_copy(M.at[:, pl.ds(gy * depth, depth)], land, own_sem)
    own.start()

    def pass_x(block, carry):
        at = [pl.ds(block * 128 + r, 8, stride=CX) for r in range(CX)]
        u = [VEL[0, a] for a in at]
        for k in range(NF):
            flux = [fo[k, a] for a in at]
            if k == 4:
                flux = [flux[r] + PR[at[r]] for r in range(CX)]
            flux = [flux[r] * u[r] for r in range(CX)]
            if k == 1:
                flux = [flux[r] + PR[at[r]] for r in range(CX)]
            for r in range(CX):
                result = ro[k, at[r]]
                for m in range(1, 5):
                    if r + m < CX and r - m >= 0:
                        result = result - (STEP * C[m - 1]) * (flux[r + m] - flux[r - m])
                    elif r + m < CX:
                        result = result - (STEP * C[m - 1]) * flux[r + m]
                    elif r - m >= 0:
                        result = result + (STEP * C[m - 1]) * flux[r - m]
                ro[k, at[r]] = result
        return carry

    lax.fori_loop(0, NZ // 8, pass_x, 0)

    def pass_z(i, carry):
        first, tile = lax.div(i, 2) * 8, lax.rem(i, 2) * 8
        at = [
            pl.ds(pl.multiple_of(lax.rem(first + (j + NZ - 4), NZ) * CX + tile, 8), 8) for j in range(16)
        ]
        w = [VEL[2, a] for a in at]
        for k in range(NF):
            flux = [fo[k, a] for a in at]
            if k == 4:
                flux = [flux[j] + PR[at[j]] for j in range(16)]
            flux = [flux[j] * w[j] for j in range(16)]
            if k == 3:
                flux = [flux[j] + PR[at[j]] for j in range(16)]
            for j in range(4, 12):
                result = ro[k, at[j]]
                for m in range(1, 5):
                    result = result - (STEP * C[m - 1]) * (flux[j + m] - flux[j - m])
                ro[k, at[j]] = result
        return carry

    lax.fori_loop(0, NZ // 4, pass_z, 0)

    def pass_y(half, carry):
        rows = pl.ds(pl.multiple_of(half * HALF, HALF), HALF)
        edges = jnp.concatenate([yr[1], yr[0]], axis=1)
        for k in range(NF):
            value, v = fo[k, rows], VEL[1, rows]
            flux = (value + PR[rows]) * v if k == 4 else value * v
            flux = flux + PR[rows] if k == 2 else flux
            high = flux.astype(BF16)
            rest = (flux - high.astype(F32)).astype(BF16)
            slope = jnp.dot(jnp.concatenate([high, rest], axis=1), wd[...], preferred_element_type=F32)
            slope = slope + jnp.dot(edges, wu[2 * k + half], preferred_element_type=F32)
            result = ro[k, rows] - (STEP / 840.0) * slope
            ro[k, rows] = result
            fo[k, rows] = value + WEIGHT * result
        return carry

    lax.fori_loop(0, 2, pass_y, 0)

    def pass_edge(block, carry):
        for side in range(2):
            copy = x_copy(side, block)
            copy.wait_recv()
            sign = STEP if side == 1 else -STEP
            for k in range(NF):
                q = [xr[side, block, pl.ds((4 * k + n) * 16, 16)].astype(F32) for n in range(4)]
                for cell in range(4):
                    change = None
                    for n in range(4 - cell):
                        term = (sign * C[n + cell]) * q[n]
                        change = term if change is None else change + term
                    at = pl.ds(block * 256 + (cell if side == 1 else 15 - cell), 16, stride=CX)
                    ro[k, at] = ro[k, at] + change
                    fo[k, at] = fo[k, at] + WEIGHT * change
        return carry

    lax.fori_loop(0, 3, pass_edge, 0)

    for copy in xp_copy + dg_copy + y_copy:
        copy.wait_send()
    for side in range(2):
        for block in range(3):
            x_copy(side, block).wait_send()
    own.wait()
    for d in range(1, 8):
        m_copy(d).wait()


def per_device(fields, register):
    inner, edge = lane_weights()
    flat = lambda a: a.reshape(NF, ROWS, LY)
    any_space, vmem = pl.BlockSpec(memory_space=pl.ANY), pl.BlockSpec(memory_space=pltpu.VMEM)
    dma = pltpu.SemaphoreType.DMA
    big = jax.ShapeDtypeStruct((NF, ROWS, LY), F32)
    fields_next, register_next, metrics = pl.pallas_call(
        kernel,
        out_shape=(
            pltpu.VMEM(big.shape, big.dtype),
            pltpu.VMEM(big.shape, big.dtype),
            jax.ShapeDtypeStruct((5, 6, CX, 1024), BF16),
        ),
        in_specs=[any_space, any_space, vmem, vmem],
        out_specs=(vmem, vmem, any_space),
        scratch_shapes=[
            pltpu.VMEM((3, ROWS, LY), F32),
            pltpu.VMEM((ROWS, LY), F32),
            pltpu.VMEM((4, NZ * 32, LY), F32),
            pltpu.VMEM((NZ * 32, LY), F32),
            pltpu.VMEM((3, ROWS, LY), F32),
            pltpu.VMEM((3, 24, LY), F32),
            pltpu.VMEM((ROWS, LY), F32),
            pltpu.VMEM((ROWS, LY), F32),
            pltpu.VMEM((5, NZ, CX, LY), BF16),
            pltpu.VMEM((2, 5, NZ, LY), BF16),
            pltpu.VMEM((2, 5, NZ, LY), BF16),
            pltpu.VMEM((4, 16, LY), BF16),
            pltpu.VMEM((4, 16, LY), BF16),
            pltpu.VMEM((2, HALF, LY), BF16),
            pltpu.VMEM((2, HALF, LY), BF16),
            pltpu.VMEM((2, 3, NF * 64, LY), BF16),
            pltpu.VMEM((2, 3, NF * 64, LY), BF16),
            dma((5,)),
            dma((2,)),
            dma((2,)),
            dma((4,)),
            dma((4,)),
            dma((2,)),
            dma((2,)),
            dma((2, 3)),
            dma((2, 3)),
            dma((8,)),
            dma((8,)),
            dma(()),
        ],
        compiler_params=pltpu.CompilerParams(collective_id=0, has_side_effects=True, vmem_limit_bytes=44 << 20),
    )(flat(fields), flat(register), jnp.asarray(inner), jnp.asarray(edge))
    shape = fields.shape
    return fields_next.reshape(shape), register_next.reshape(shape), metrics


def solution(mesh):
    in_specs = (P(None, None, "gx", "gy"), P(None, None, "gx", "gy"))
    out_specs = (P(None, None, "gx", "gy"), P(None, None, "gx", "gy"), P(None, "gy", "gx", None))
    return jax.shard_map(per_device, mesh=mesh, in_specs=in_specs, out_specs=out_specs, check_vma=False)
```

```python
import jax
import jax.numpy as jnp
import numpy as np
from jax import lax
from jax.experimental import pallas as pl
from jax.experimental.pallas import tpu as pltpu
from jax.sharding import PartitionSpec as P

MESH = pl.DeviceIdType.MESH
F32, BF16 = jnp.float32, jnp.bfloat16
DECAY = -0.4178904745
STEP = 0.25
WEIGHT = 0.3792103129
C = (0.8, -0.2, 4.0 / 105.0, -1.0 / 280.0)
MOLAR_MASS = (2.0, 32.0, 16.0, 17.0, 18.0, 1.0, 33.0, 34.0, 28.0)
FORMATION_HEAT = (0.0, 0.0, 2.0, 0.3, -1.5, 3.0, 0.1, -0.4, 0.0)
REACTIONS = (
    (5, 1, (2, 3), 40.0, 2.0),
    (2, 0, (5, 3), 30.0, 1.2),
    (3, 0, (5, 4), 25.0, 0.8),
    (2, 4, (3, 3), 10.0, 1.6),
    (5, 1, (6,), 15.0, 0.2),
    (6, 5, (3, 3), 20.0, 0.3),
    (6, 6, (7, 1), 12.0, 0.4),
    (7, 8, (3, 3, 8), 8.0, 1.8),
)
NF, NZ, CX, LY = 14, 48, 16, 128
ROWS = NZ * CX
HALF = ROWS // 2


def make_table():
    table = np.zeros((14, 8))
    for column, record in enumerate(REACTIONS):
        change = np.zeros(9)
        change[record[0]] -= 1.0
        change[record[1]] -= 1.0
        for product in record[2]:
            change[product] += 1.0
        for species in range(9):
            mass_change = MOLAR_MASS[species] / 18.0 * change[species]
            table[5 + species, column] = mass_change
            table[4, column] -= FORMATION_HEAT[species] * mass_change
    return table


TABLE = make_table()


WHOLE = (672.0, -168.0, 32.0, -3.0)


def fill_weights(wd, wu):
    gap = lax.broadcasted_iota(jnp.int32, (LY, LY), 0) - lax.broadcasted_iota(jnp.int32, (LY, LY), 1)
    inner = jnp.zeros((LY, LY), F32)
    for m in range(1, 5):
        inner = jnp.where(gap == m, WHOLE[m - 1], jnp.where(gap == -m, -WHOLE[m - 1], inner))
    wd[0:LY] = inner.astype(BF16)
    wd[LY : 2 * LY] = inner.astype(BF16)

    def clear(i, carry):
        wu[i] = jnp.zeros((2 * LY, LY), BF16)
        return carry

    lax.fori_loop(0, 2 * NF, clear, 0)
    row, lane = lax.broadcasted_iota(jnp.int32, (16, LY), 0), lax.broadcasted_iota(jnp.int32, (16, LY), 1)
    tiles = []
    for offset in range(0, 16, 4):
        layer = row - offset
        low, high = jnp.zeros((16, LY), F32), jnp.zeros((16, LY), F32)
        for n in range(4):
            low = jnp.where(layer - lane == n, -WHOLE[3 - n], low)
            high = jnp.where(layer + (LY - 1) - lane == n, WHOLE[n], high)
        valid = (layer >= 0) & (layer < 4)
        tiles.append([jnp.where(valid, t, 0.0).astype(BF16) for t in (low, high)])
    for k in range(NF):
        for half in range(2):
            base = 8 * k + 4 * half
            first = base // 16 * 16
            wu[2 * k + half, first : first + 16] = tiles[base % 16 // 4][0]
            wu[2 * k + half, LY + first : LY + first + 16] = tiles[base % 16 // 4][1]


def rounded(x):
    return x.astype(BF16).astype(F32)


def shaped(h):
    q1 = rounded(h[0])
    e1 = q1 - h[0]
    q2 = rounded(h[1] + 4.0 * e1)
    left = C[0] * e1 + C[1] * (q2 - h[1])
    q3 = rounded(h[2] - left * (1.0 / C[2]))
    left = left + C[2] * (q3 - h[2])
    return q1, q2, q3, h[3] - left * (1.0 / C[3])


def shaped_lanes(x, layer, turn):
    roll = lambda a, n: pltpu.roll(a, (turn * n) % LY, 1)
    q1 = rounded(x)
    e1 = jnp.where(layer == 0, q1 - x, 0.0)
    q2 = rounded(x + 4.0 * roll(e1, 1))
    e2 = jnp.where(layer == 1, q2 - x, 0.0)
    left = C[0] * roll(e1, 1) + C[1] * e2
    left = roll(left, 1)
    q3 = rounded(x - left * (1.0 / C[2]))
    left = roll(jnp.where(layer == 2, left + C[2] * (q3 - x), 0.0), 1)
    q4 = rounded(x - left * (1.0 / C[3]))
    return jnp.where(layer == 0, q1, jnp.where(layer == 1, q2, jnp.where(layer == 2, q3, q4)))


def loop(count, body, unroll):
    def several(i, carry):
        for j in range(unroll):
            body(i * unroll + j, j)
        return carry

    lax.fori_loop(0, count // unroll, several, 0)


def kernel(
    f_hbm, r_hbm, fo, ro, mo,
    wd, wu, VEL, PR, PX, TX, YH, NS, NZS, CV, M,
    xps, xpr, dgs, dgr, yps, ypr, PY, ys, yr, xs, xr,
    load_sem, xp_ss, xp_rs, dg_ss, dg_rs, yp_ss, yp_rs, y_ss, y_rs, x_ss, x_rs, m_ss, m_rs, own_sem,
):
    gx, gy = lax.axis_index("gx"), lax.axis_index("gy")
    nx, ny = lax.axis_size("gx"), lax.axis_size("gy")
    gxs = (lax.rem(gx + nx - 1, nx), lax.rem(gx + 1, nx))
    gys = (lax.rem(gy + ny - 1, ny), lax.rem(gy + 1, ny))

    barrier = pltpu.get_barrier_semaphore()
    partners = [(gxs[0], gy), (gxs[1], gy)]
    partners += [(gxs[a], gys[b]) for a in range(2) for b in range(2)]
    partners += [(gx, lax.rem(gy + d, ny)) for d in range(1, ny)]
    for partner in partners:
        pl.semaphore_signal(barrier, 1, device_id=partner, device_id_type=MESH)

    loads = [
        pltpu.make_async_copy(f_hbm.at[:, pl.ds(n * 256, 256)], fo.at[:, pl.ds(n * 256, 256)], load_sem.at[n])
        for n in range(3)
    ]
    loads.append(pltpu.make_async_copy(r_hbm, ro, load_sem.at[3]))
    for load in loads:
        load.start()

    def remote(src, dst, ss, rs, device):
        return pltpu.make_async_remote_copy(
            src_ref=src, dst_ref=dst, send_sem=ss, recv_sem=rs, device_id=device, device_id_type=MESH
        )

    def primitive(z, _):
        rows = pl.ds(pl.multiple_of(z * CX, CX), CX)
        mine = pl.ds(pl.multiple_of(z * 32 + 8, 8), CX)
        inverse = 1.0 / fo[0, rows]
        moment = [fo[1 + d, rows] for d in range(3)]
        speed = [m * inverse for m in moment]
        PR[rows] = 0.4 * (fo[4, rows] - 0.5 * (moment[0] * speed[0] + moment[1] * speed[1] + moment[2] * speed[2]))
        PX[0, mine] = rounded(4.0 * (fo[9, rows] * inverse))
        for d in range(3):
            VEL[d, rows] = speed[d]
            PX[1 + d, mine] = rounded(speed[d])

    def x_copy(side, block):
        return remote(
            xs.at[side, block], xr.at[side, block], x_ss.at[side, block], x_rs.at[side, block], (gxs[side], gy)
        )

    def pack_x(block):
        for side in range(2):
            at = [pl.ds(block * 256 + (n if side == 0 else 15 - n), 16, stride=CX) for n in range(4)]
            u = [VEL[0, a] for a in at]
            for k in range(NF):
                h = []
                for n in range(4):
                    flux = fo[k, at[n]]
                    flux = (flux + PR[at[n]]) * u[n] if k == 4 else flux * u[n]
                    h.append(flux + PR[at[n]] if k == 1 else flux)
                for n, q in enumerate(shaped(h)):
                    xs[side, block, pl.ds((4 * k + n) * 16, 16)] = q.astype(BF16)

    def send_x(block):
        for side in range(2):
            x_copy(side, block).start()

    loads[0].wait()
    loop(16, primitive, 4)
    pack_x(0)
    pl.semaphore_wait(barrier, len(partners))
    send_x(0)
    loads[1].wait()
    loads[2].wait()
    loop(32, lambda z, _: primitive(z + 16, _), 4)

    lane48 = lax.broadcasted_iota(jnp.int32, (NZ, LY), 1)
    eye48 = lane48 == lax.broadcasted_iota(jnp.int32, (NZ, LY), 0)
    for side, (near, far) in enumerate(((0, 1), (15, 14))):
        xps[side, 0] = PX[0, pl.ds(8 + near, NZ, stride=32)].astype(BF16)
        xps[side, 1] = PX[0, pl.ds(8 + far, NZ, stride=32)].astype(BF16)
        for d in range(3):
            xps[side, 2 + d] = PX[1 + d, pl.ds(8 + near, NZ, stride=32)].astype(BF16)
        edge = PX[0, pl.ds(8 + near, NZ, stride=32)]
        for along, lane in enumerate((0, LY - 1)):
            column = jnp.sum(jnp.where(lane48 == lane, edge, 0.0), axis=1, keepdims=True)
            line = jnp.sum(jnp.where(eye48, column, 0.0), axis=0, keepdims=True)
            dgs[2 * side + along] = jnp.broadcast_to(line, (16, LY)).astype(BF16)

    xp_copy = [remote(xps.at[s], xpr.at[s], xp_ss.at[s], xp_rs.at[s], (gxs[s], gy)) for s in range(2)]
    dg_copy = [
        remote(dgs.at[n], dgr.at[n], dg_ss.at[n], dg_rs.at[n], (gxs[n // 2], gys[n % 2])) for n in range(4)
    ]
    for copy in xp_copy + dg_copy:
        copy.start()

    lane = lax.broadcasted_iota(jnp.int32, (CX, LY), 1)

    def pack_probe(block, _):
        packed = []
        for half in range(2):
            total = None
            for j in range(8):
                mine = pl.ds(pl.multiple_of((half * (NZ // 2) + block * 8 + j) * 32 + 8, 8), CX)
                face = PX[0, mine]
                for d in range(3):
                    speed = PX[1 + d, mine]
                    face = jnp.where(lane == 2 + d, pltpu.roll(speed, 2 + d, 1), face)
                    face = jnp.where(lane == 125 - d, pltpu.roll(speed, LY - 2 - d, 1), face)
                face = pltpu.roll(face, (16 * j + 8) % LY, 1)
                total = face if total is None else jnp.where((lane >> 4) == j, face, total)
            packed.append(total)
        rows = pl.ds(pl.multiple_of(block * CX, CX), CX)
        first = (lane & 15) < 8
        yps[0, rows] = jnp.where(first, pltpu.roll(packed[0], LY - 8, 1), packed[1]).astype(BF16)
        yps[1, rows] = jnp.where(first, packed[0], pltpu.roll(packed[1], 8, 1)).astype(BF16)

    loop(3, pack_probe, 1)
    yp_copy = [remote(yps.at[s], ypr.at[s], yp_ss.at[s], yp_rs.at[s], (gx, gys[s])) for s in range(2)]
    for copy in yp_copy:
        copy.start()
    def later_x(block, carry):
        pack_x(block)
        send_x(block)
        return carry

    lax.fori_loop(1, 3, later_x, 0)

    place = lane & 7
    layer = lane & 3

    def pack_y(i, _):
        packed = []
        for half in range(2):
            rows = pl.ds(pl.multiple_of(half * HALF + i * CX, CX), CX)
            v, p = VEL[1, rows], PR[rows]
            total = jnp.zeros((CX, LY), F32)
            for slot in range(NF):
                flux = fo[slot, rows]
                flux = (flux + p) * v if slot == 4 else flux * v
                flux = flux + p if slot == 2 else flux
                total = jnp.where((lane >> 3) == slot, pltpu.roll(flux, (4 + 8 * slot) % LY, 1), total)
            packed.append(total)
        rows = pl.ds(pl.multiple_of(i * CX, CX), CX)
        PY[0, rows] = jnp.where(place < 4, pltpu.roll(packed[0], LY - 4, 1), packed[1])
        PY[1, rows] = jnp.where(place < 4, packed[0], pltpu.roll(packed[1], 4, 1))

    loop(NZ // 2, pack_y, 3)
    deep = lax.broadcasted_iota(jnp.int32, (HALF // 4, LY), 1) & 3

    def shape_y(i, _):
        rows = pl.ds(pl.multiple_of(i * (HALF // 4), CX), HALF // 4)
        ys[0, rows] = shaped_lanes(PY[0, rows], deep, 1).astype(BF16)
        ys[1, rows] = shaped_lanes(PY[1, rows], 3 - deep, -1).astype(BF16)

    loop(4, shape_y, 1)
    y_copy = [remote(ys.at[s], yr.at[s], y_ss.at[s], y_rs.at[s], (gx, gys[s])) for s in range(2)]
    for copy in y_copy:
        copy.start()

    fill_weights(wd, wu)

    loads[3].wait()

    def chemistry(z, _):
        rows = pl.ds(pl.multiple_of(z * CX, CX), CX)
        moles = [fo[5 + k, rows] * (18.0 / MOLAR_MASS[k]) for k in range(9)]
        total = moles[0]
        for k in range(1, 9):
            total = total + moles[k]
        cold = (0.25 * total) / PR[rows]
        rates = [
            record[3] * jnp.exp(-record[4] * cold) * (moles[record[0]] * moles[record[1]]) for record in REACTIONS
        ]
        for k in range(NF):
            result = DECAY * ro[k, rows]
            for r in range(8):
                if TABLE[k, r] != 0.0:
                    result = result + float(STEP * TABLE[k, r]) * rates[r]
            ro[k, rows] = result

    loop(NZ, chemistry, 4)

    for s in range(2):
        xp_copy[s].wait_recv()
    for side, near, far in ((1, 7, 6), (0, 24, 25)):
        PX[0, pl.ds(near, NZ, stride=32)] = xpr[side, 0].astype(F32)
        PX[0, pl.ds(far, NZ, stride=32)] = xpr[side, 1].astype(F32)
        for d in range(3):
            PX[1 + d, pl.ds(near, NZ, stride=32)] = xpr[side, 2 + d].astype(F32)
    for n in range(4):
        dg_copy[n].wait_recv()
    for side, row in ((1, 7), (0, 24)):
        corner = []
        for along in (1, 0):
            line = dgr[2 * side + along].astype(F32)[0:1]
            corner.append(jnp.sum(jnp.where(eye48, line, 0.0), axis=1, keepdims=True))
        TX[pl.ds(row, NZ, stride=32)] = jnp.where(lane48 < 64, corner[0], corner[1])
    for s in range(2):
        yp_copy[s].wait_recv()

    def turned(block, _):
        there = pl.ds(pl.multiple_of(block * CX, CX), CX)
        low, high = ypr[1, there].astype(F32), ypr[0, there].astype(F32)
        put = lambda a, source, target: pltpu.roll(a, (target - source) % LY, 1)
        for half, j in [(half, j) for half in range(2) for j in range(8)]:
            z = half * (NZ // 2) + block * 8 + j
            rows = pl.ds(pl.multiple_of(z * CX, CX), CX)
            mine = pl.ds(pl.multiple_of(z * 32 + 8, 8), CX)
            base = 16 * j + 8 * half
            s = PX[0, mine]
            t = jnp.where(lane < 64, pltpu.roll(s, 2, 1), pltpu.roll(s, LY - 2, 1))
            t = jnp.where(lane < 2, put(low, base + 6, 0), t)
            TX[mine] = jnp.where(lane >= 126, put(high, base, 126), t)
            for d in range(3):
                YH[d, rows] = jnp.where(lane < 64, put(low, base + 5 - d, 0), put(high, base + 2 + d, 127))

    loop(3, turned, 1)

    def normals(z, turn):
        above, below = lax.rem(z + 1, NZ), lax.rem(z + NZ - 1, NZ)
        rows = pl.ds(pl.multiple_of(z * CX, CX), CX)

        def wide(ref, plane, shift):
            return ref[0, pl.ds(plane * 32 + 4 + shift, 24)]

        def mine(plane, shift=0):
            return pl.ds(plane * 32 + 8 + shift, CX)

        lane24 = lax.broadcasted_iota(jnp.int32, (24, LY), 1)
        s, t = wide(PX, z, 0), TX[pl.ds(z * 32 + 4, 24)]
        behind = jnp.where(lane24 == 0, pltpu.roll(t, LY - 1, 1), pltpu.roll(s, 1, 1))
        ahead = jnp.where(lane24 == LY - 1, pltpu.roll(t, 1, 1), pltpu.roll(s, LY - 1, 1))
        grad_x = 0.5 * (wide(PX, z, 1) - wide(PX, z, -1))
        grad_y = 0.5 * (ahead - behind)
        grad_z = 0.5 * (wide(PX, above, 0) - wide(PX, below, 0))
        scale = -lax.rsqrt(jnp.maximum(grad_x * grad_x + grad_y * grad_y + grad_z * grad_z, 0.01))
        NS[turn, 0], NS[turn, 1], NS[turn, 2] = grad_x * scale, grad_y * scale, grad_z * scale
        normal = [NS[turn, d, 4:20] for d in range(3)]

        t = TX[mine(z)]
        edge_x = 0.5 * (TX[mine(z, 1)] - TX[mine(z, -1)])
        edge_y = 0.5 * (pltpu.roll(t, LY - 1, 1) - pltpu.roll(t, 1, 1))
        edge_z = 0.5 * (TX[mine(above)] - TX[mine(below)])
        edge = -edge_y * lax.rsqrt(jnp.maximum(edge_x * edge_x + edge_y * edge_y + edge_z * edge_z, 0.01))
        behind = jnp.where(lane == 0, pltpu.roll(edge, LY - 1, 1), pltpu.roll(normal[1], 1, 1))
        ahead = jnp.where(lane == LY - 1, pltpu.roll(edge, 1, 1), pltpu.roll(normal[1], LY - 1, 1))
        CV[rows] = 0.5 * (NS[turn, 0, 5:21] - NS[turn, 0, 3:19]) + 0.5 * (ahead - behind)
        NZS[rows] = normal[2]

        strain = None
        for d in range(3):
            speed, halo = PX[1 + d, mine(z)], YH[d, rows]
            behind = jnp.where(lane == 0, halo, pltpu.roll(speed, 1, 1))
            ahead = jnp.where(lane == LY - 1, halo, pltpu.roll(speed, LY - 1, 1))
            along = (
                0.5 * (PX[1 + d, mine(z, 1)] - PX[1 + d, mine(z, -1)]),
                0.5 * (ahead - behind),
                0.5 * (PX[1 + d, mine(above)] - PX[1 + d, mine(below)]),
            )
            inner = normal[0] * along[0] + normal[1] * along[1] + normal[2] * along[2]
            term = along[d] - normal[d] * inner
            strain = term if strain is None else strain + term
        for d in range(3):
            M[d, z] = normal[d].astype(BF16)
        M[4, z] = strain.astype(BF16)

    loop(NZ, normals, 3)

    depth = NZ // 8

    def curve(z, _):
        above, below = lax.rem(z + 1, NZ), lax.rem(z + NZ - 1, NZ)
        at = lambda plane: pl.ds(pl.multiple_of(plane * CX, CX), CX)
        M[3, z] = (CV[at(z)] + 0.5 * (NZS[at(above)] - NZS[at(below)])).astype(BF16)

    loop(NZ, curve, 6)
    land = mo.at[:, :, :, pl.ds(pl.multiple_of(gy * LY, LY), LY)]

    def m_copy(d):
        target = lax.rem(gy + d, ny)
        return remote(M.at[:, pl.ds(target * depth, depth)], land, m_ss.at[d], m_rs.at[d], (gx, target))

    for d in range(1, 8):
        m_copy(d).start()
    own = pltpu.make_async_copy(M.at[:, pl.ds(gy * depth, depth)], land, own_sem)
    own.start()

    def pass_z(i, carry):
        first, tile = lax.div(i, 2) * 8, lax.rem(i, 2) * 8
        at = [
            pl.ds(pl.multiple_of(lax.rem(first + (j + NZ - 4), NZ) * CX + tile, 8), 8) for j in range(16)
        ]
        w = [VEL[2, a] for a in at]
        for k in range(NF):
            flux = [fo[k, a] for a in at]
            if k == 4:
                flux = [flux[j] + PR[at[j]] for j in range(16)]
            flux = [flux[j] * w[j] for j in range(16)]
            if k == 3:
                flux = [flux[j] + PR[at[j]] for j in range(16)]
            before = [ro[k, a] for a in at[4:12]]
            after = []
            for j in range(4, 12):
                change = (STEP * C[0]) * (flux[j - 1] - flux[j + 1])
                for m in range(2, 5):
                    change = change + (STEP * C[m - 1]) * (flux[j - m] - flux[j + m])
                after.append(before[j - 4] + change)
            for j in range(4, 12):
                ro[k, at[j]] = after[j - 4]
        return carry

    lax.fori_loop(0, NZ // 4, pass_z, 0)

    def pass_x(block, carry):
        for side in range(2):
            x_copy(side, block).wait_recv()
        for part in range(2):
            at = [pl.ds(block * 256 + part * 128 + r, 8, stride=CX) for r in range(CX)]
            u = [VEL[0, a] for a in at]
            for k in range(NF):
                flux = [fo[k, a] for a in at]
                if k == 4:
                    flux = [flux[r] + PR[at[r]] for r in range(CX)]
                flux = [flux[r] * u[r] for r in range(CX)]
                if k == 1:
                    flux = [flux[r] + PR[at[r]] for r in range(CX)]
                low, high = [
                    [
                        xr[side, block, pl.ds((4 * k + n) * 16, 16)].astype(F32)[8 * part : 8 * part + 8]
                        for n in range(4)
                    ]
                    for side in (1, 0)
                ]
                flux = low[::-1] + flux + high
                before = [ro[k, a] for a in at]
                after = []
                for r in range(CX):
                    change = (STEP * C[0]) * (flux[r + 3] - flux[r + 5])
                    for m in range(2, 5):
                        change = change + (STEP * C[m - 1]) * (flux[r + 4 - m] - flux[r + 4 + m])
                    after.append(before[r] + change)
                for r in range(CX):
                    ro[k, at[r]] = after[r]
        return carry

    lax.fori_loop(0, 3, pass_x, 0)

    for s in range(2):
        y_copy[s].wait_recv()

    def pass_y(half, carry):
        rows = pl.ds(pl.multiple_of(half * HALF, HALF), HALF)
        edges = jnp.concatenate([yr[1], yr[0]], axis=1)
        for k in range(NF):
            value, v = fo[k, rows], VEL[1, rows]
            flux = (value + PR[rows]) * v if k == 4 else value * v
            flux = flux + PR[rows] if k == 2 else flux
            high = flux.astype(BF16)
            rest = (flux - high.astype(F32)).astype(BF16)
            slope = jnp.dot(jnp.concatenate([high, rest], axis=1), wd[...], preferred_element_type=F32)
            slope = slope + jnp.dot(edges, wu[2 * k + half], preferred_element_type=F32)
            result = ro[k, rows] - (STEP / 840.0) * slope
            ro[k, rows] = result
        return carry

    lax.fori_loop(0, 2, pass_y, 0)

    for copy in xp_copy + dg_copy + yp_copy + y_copy:
        copy.wait_send()
    for side in range(2):
        for block in range(3):
            x_copy(side, block).wait_send()
    own.wait()
    for d in range(1, 8):
        m_copy(d).wait()


def place_out(f_in, r_in, m_in, f_out, r_out, m_out, new, sem):
    copies = [
        pltpu.make_async_copy(m_in, m_out, sem.at[0]),
        pltpu.make_async_copy(r_in.at[pl.ds(0, 7)], r_out.at[pl.ds(0, 7)], sem.at[1]),
        pltpu.make_async_copy(r_in.at[pl.ds(7, 7)], r_out.at[pl.ds(7, 7)], sem.at[2]),
    ]
    for copy in copies:
        copy.start()
    for part in range(7):
        for k in (2 * part, 2 * part + 1):

            def update(i, _, k=k):
                rows = pl.ds(pl.multiple_of(i * 192, 192), 192)
                new[k, rows] = f_in[k, rows] + WEIGHT * r_in[k, rows]

            loop(4, update, 1)
        at = pl.ds(2 * part, 2)
        copies.append(pltpu.make_async_copy(new.at[at], f_out.at[at], sem.at[3 + part]))
        copies[-1].start()
    for copy in copies:
        copy.wait()


def per_device(fields, register):
    flat = lambda a: a.reshape(NF, ROWS, LY)
    any_space, vmem = pl.BlockSpec(memory_space=pl.ANY), pl.BlockSpec(memory_space=pltpu.VMEM)
    hbm = pl.BlockSpec(memory_space=pltpu.HBM)
    dma = pltpu.SemaphoreType.DMA
    big = jax.ShapeDtypeStruct((NF, ROWS, LY), F32)
    fields_next, register_next, metrics = pl.pallas_call(
        kernel,
        out_shape=(
            pltpu.VMEM(big.shape, big.dtype),
            pltpu.VMEM(big.shape, big.dtype),
            pltpu.VMEM((5, 6, CX, 1024), BF16),
        ),
        in_specs=[hbm] * 2,
        out_specs=(vmem, vmem, vmem),
        scratch_shapes=[
            pltpu.VMEM((2 * LY, LY), BF16),
            pltpu.VMEM((2 * NF, 2 * LY, LY), BF16),
            pltpu.VMEM((3, ROWS, LY), F32),
            pltpu.VMEM((ROWS, LY), F32),
            pltpu.VMEM((4, NZ * 32, LY), F32),
            pltpu.VMEM((NZ * 32, LY), F32),
            pltpu.VMEM((3, ROWS, LY), F32),
            pltpu.VMEM((3, 3, 24, LY), F32),
            pltpu.VMEM((ROWS, LY), F32),
            pltpu.VMEM((ROWS, LY), F32),
            pltpu.VMEM((5, NZ, CX, LY), BF16),
            pltpu.VMEM((2, 5, NZ, LY), BF16),
            pltpu.VMEM((2, 5, NZ, LY), BF16),
            pltpu.VMEM((4, 16, LY), BF16),
            pltpu.VMEM((4, 16, LY), BF16),
            pltpu.VMEM((2, 48, LY), BF16),
            pltpu.VMEM((2, 48, LY), BF16),
            pltpu.VMEM((2, HALF, LY), F32),
            pltpu.VMEM((2, HALF, LY), BF16),
            pltpu.VMEM((2, HALF, LY), BF16),
            pltpu.VMEM((2, 3, NF * 64, LY), BF16),
            pltpu.VMEM((2, 3, NF * 64, LY), BF16),
            dma((4,)),
            dma((2,)),
            dma((2,)),
            dma((4,)),
            dma((4,)),
            dma((2,)),
            dma((2,)),
            dma((2,)),
            dma((2,)),
            dma((2, 3)),
            dma((2, 3)),
            dma((8,)),
            dma((8,)),
            dma(()),
        ],
        compiler_params=pltpu.CompilerParams(collective_id=0, has_side_effects=True, vmem_limit_bytes=40 << 20),
    )(flat(fields), flat(register))
    small = jax.ShapeDtypeStruct(metrics.shape, BF16)
    fields_next, register_next, metrics = pl.pallas_call(
        place_out,
        out_shape=(big, big, small),
        in_specs=[vmem] * 3,
        out_specs=(any_space,) * 3,
        scratch_shapes=[pltpu.VMEM(big.shape, F32), dma((10,))],
        compiler_params=pltpu.CompilerParams(vmem_limit_bytes=8 << 20),
    )(*(pltpu.with_memory_space_constraint(a, pltpu.VMEM) for a in (fields_next, register_next, metrics)))
    shape = fields.shape
    return fields_next.reshape(shape), register_next.reshape(shape), metrics


def solution(mesh):
    in_specs = (P(None, None, "gx", "gy"), P(None, None, "gx", "gy"))
    out_specs = (P(None, None, "gx", "gy"), P(None, None, "gx", "gy"), P(None, "gy", "gx", None))
    return jax.shard_map(per_device, mesh=mesh, in_specs=in_specs, out_specs=out_specs, check_vma=False)
```

```python
import jax
import jax.numpy as jnp
import numpy as np
from jax import lax
from jax.experimental import pallas as pl
from jax.experimental.pallas import tpu as pltpu
from jax.sharding import PartitionSpec as P

MESH = pl.DeviceIdType.MESH
F32, BF16 = jnp.float32, jnp.bfloat16
DECAY = -0.4178904745
STEP = 0.25
WEIGHT = 0.3792103129
C = (0.8, -0.2, 4.0 / 105.0, -1.0 / 280.0)
MOLAR_MASS = (2.0, 32.0, 16.0, 17.0, 18.0, 1.0, 33.0, 34.0, 28.0)
FORMATION_HEAT = (0.0, 0.0, 2.0, 0.3, -1.5, 3.0, 0.1, -0.4, 0.0)
REACTIONS = (
    (5, 1, (2, 3), 40.0, 2.0),
    (2, 0, (5, 3), 30.0, 1.2),
    (3, 0, (5, 4), 25.0, 0.8),
    (2, 4, (3, 3), 10.0, 1.6),
    (5, 1, (6,), 15.0, 0.2),
    (6, 5, (3, 3), 20.0, 0.3),
    (6, 6, (7, 1), 12.0, 0.4),
    (7, 8, (3, 3, 8), 8.0, 1.8),
)
NF, NZ, CX, LY = 14, 48, 16, 128
ROWS = NZ * CX
HALF = ROWS // 2


def make_table():
    table = np.zeros((14, 8))
    for column, record in enumerate(REACTIONS):
        change = np.zeros(9)
        change[record[0]] -= 1.0
        change[record[1]] -= 1.0
        for product in record[2]:
            change[product] += 1.0
        for species in range(9):
            mass_change = MOLAR_MASS[species] / 18.0 * change[species]
            table[5 + species, column] = mass_change
            table[4, column] -= FORMATION_HEAT[species] * mass_change
    return table


TABLE = make_table()


WHOLE = (672.0, -168.0, 32.0, -3.0)


def fill_weights(wd, wu):
    gap = lax.broadcasted_iota(jnp.int32, (LY, LY), 0) - lax.broadcasted_iota(jnp.int32, (LY, LY), 1)
    inner = jnp.zeros((LY, LY), F32)
    for m in range(1, 5):
        inner = jnp.where(gap == m, WHOLE[m - 1], jnp.where(gap == -m, -WHOLE[m - 1], inner))
    wd[0:LY] = inner.astype(BF16)
    wd[LY : 2 * LY] = inner.astype(BF16)

    def clear(i, carry):
        wu[i] = jnp.zeros((2 * LY, LY), BF16)
        return carry

    lax.fori_loop(0, 2 * NF, clear, 0)
    row, lane = lax.broadcasted_iota(jnp.int32, (16, LY), 0), lax.broadcasted_iota(jnp.int32, (16, LY), 1)
    tiles = []
    for offset in range(0, 16, 4):
        layer = row - offset
        low, high = jnp.zeros((16, LY), F32), jnp.zeros((16, LY), F32)
        for n in range(4):
            low = jnp.where(layer - lane == n, -WHOLE[3 - n], low)
            high = jnp.where(layer + (LY - 1) - lane == n, WHOLE[n], high)
        valid = (layer >= 0) & (layer < 4)
        tiles.append([jnp.where(valid, t, 0.0).astype(BF16) for t in (low, high)])
    for k in range(NF):
        for half in range(2):
            base = 8 * k + 4 * half
            first = base // 16 * 16
            wu[2 * k + half, first : first + 16] = tiles[base % 16 // 4][0]
            wu[2 * k + half, LY + first : LY + first + 16] = tiles[base % 16 // 4][1]


def rounded(x):
    return x.astype(BF16).astype(F32)


KNOWN = {(2, 0): 3, (3, 0): 4, (9, 0): 0, (9, 1): 1}
SENT = [(k, n) for k in range(NF) for n in range(4) if (k, n) not in KNOWN]


def known_flux(k, mass, probe):
    return mass * probe * 0.25 if k == 9 else mass * probe


def shaped(h, given=()):
    q1 = given[0] if len(given) > 0 else rounded(h[0])
    e1 = q1 - h[0]
    q2 = given[1] if len(given) > 1 else rounded(h[1] + 4.0 * e1)
    left = C[0] * e1 + C[1] * (q2 - h[1])
    q3 = rounded(h[2] - left * (1.0 / C[2]))
    left = left + C[2] * (q3 - h[2])
    return q1, q2, q3, h[3] - left * (1.0 / C[3])


def shaped_lanes(x, layer, turn):
    roll = lambda a, n: pltpu.roll(a, (turn * n) % LY, 1)
    q1 = rounded(x)
    e1 = jnp.where(layer == 0, q1 - x, 0.0)
    q2 = rounded(x + 4.0 * roll(e1, 1))
    e2 = jnp.where(layer == 1, q2 - x, 0.0)
    left = C[0] * roll(e1, 1) + C[1] * e2
    left = roll(left, 1)
    q3 = rounded(x - left * (1.0 / C[2]))
    left = roll(jnp.where(layer == 2, left + C[2] * (q3 - x), 0.0), 1)
    q4 = rounded(x - left * (1.0 / C[3]))
    return jnp.where(layer == 0, q1, jnp.where(layer == 1, q2, jnp.where(layer == 2, q3, q4)))


def loop(count, body, unroll):
    def several(i, carry):
        for j in range(unroll):
            body(i * unroll + j, j)
        return carry

    lax.fori_loop(0, count // unroll, several, 0)


def kernel(
    f_hbm, r_hbm, fo, ro, mo,
    wd, wu, VEL, PR, PX, TX, YH, NS, NZS, CV, M,
    xps, xpr, dgs, dgr, yps, ypr, PY, ys, yr, xs, xr,
    load_sem, xp_ss, xp_rs, dg_ss, dg_rs, yp_ss, yp_rs, y_ss, y_rs, x_ss, x_rs, m_ss, m_rs, own_sem,
):
    gx, gy = lax.axis_index("gx"), lax.axis_index("gy")
    nx, ny = lax.axis_size("gx"), lax.axis_size("gy")
    gxs = (lax.rem(gx + nx - 1, nx), lax.rem(gx + 1, nx))
    gys = (lax.rem(gy + ny - 1, ny), lax.rem(gy + 1, ny))

    barrier = pltpu.get_barrier_semaphore()
    partners = [(gxs[0], gy), (gxs[1], gy)]
    partners += [(gxs[a], gys[b]) for a in range(2) for b in range(2)]
    partners += [(gx, lax.rem(gy + d, ny)) for d in range(1, ny)]
    for partner in partners:
        pl.semaphore_signal(barrier, 1, device_id=partner, device_id_type=MESH)

    loads = [
        pltpu.make_async_copy(f_hbm.at[:, pl.ds(n * 256, 256)], fo.at[:, pl.ds(n * 256, 256)], load_sem.at[n])
        for n in range(3)
    ]
    loads.append(pltpu.make_async_copy(r_hbm, ro, load_sem.at[3]))
    for load in loads:
        load.start()

    def remote(src, dst, ss, rs, device):
        return pltpu.make_async_remote_copy(
            src_ref=src, dst_ref=dst, send_sem=ss, recv_sem=rs, device_id=device, device_id_type=MESH
        )

    def primitive(z, _):
        rows = pl.ds(pl.multiple_of(z * CX, CX), CX)
        mine = pl.ds(pl.multiple_of(z * 32 + 8, 8), CX)
        inverse = 1.0 / fo[0, rows]
        moment = [fo[1 + d, rows] for d in range(3)]
        speed = [m * inverse for m in moment]
        PR[rows] = 0.4 * (fo[4, rows] - 0.5 * (moment[0] * speed[0] + moment[1] * speed[1] + moment[2] * speed[2]))
        PX[0, mine] = rounded(4.0 * (fo[9, rows] * inverse))
        for d in range(3):
            VEL[d, rows] = speed[d]
            PX[1 + d, mine] = rounded(speed[d])

    def x_copy(side, block):
        return remote(
            xs.at[side, block], xr.at[side, block], x_ss.at[side, block], x_rs.at[side, block], (gxs[side], gy)
        )

    def pack_x(block):
        for side in range(2):
            at = [pl.ds(block * 256 + (n if side == 0 else 15 - n), 16, stride=CX) for n in range(4)]
            u = [VEL[0, a] for a in at]
            for k in range(NF):
                h = []
                for n in range(4):
                    flux = fo[k, at[n]]
                    flux = (flux + PR[at[n]]) * u[n] if k == 4 else flux * u[n]
                    h.append(flux + PR[at[n]] if k == 1 else flux)
                given = []
                for n in range(2):
                    if (k, n) in KNOWN:
                        row = n if side == 0 else 15 - n
                        probe = PX[{2: 2, 3: 3, 9: 0}[k], pl.ds(block * 512 + 8 + row, 16, stride=32)]
                        given.append(known_flux(k, mass[n], probe))
                q = shaped(h, given)
                mass = q[:2] if k == 0 else mass
                for n in range(4):
                    if (k, n) not in KNOWN:
                        xs[side, block, pl.ds(SENT.index((k, n)) * 16, 16)] = q[n].astype(BF16)

    def send_x(block):
        for side in range(2):
            x_copy(side, block).start()

    loads[0].wait()
    loop(16, primitive, 4)
    pl.semaphore_wait(barrier, len(partners))
    loads[1].wait()
    loads[2].wait()
    loop(32, lambda z, _: primitive(z + 16, _), 4)

    lane48 = lax.broadcasted_iota(jnp.int32, (NZ, LY), 1)
    eye48 = lane48 == lax.broadcasted_iota(jnp.int32, (NZ, LY), 0)
    for side, (near, far) in enumerate(((0, 1), (15, 14))):
        xps[side, 0] = PX[0, pl.ds(8 + near, NZ, stride=32)].astype(BF16)
        xps[side, 1] = PX[0, pl.ds(8 + far, NZ, stride=32)].astype(BF16)
        for d in range(3):
            xps[side, 2 + d] = PX[1 + d, pl.ds(8 + near, NZ, stride=32)].astype(BF16)
        edge = PX[0, pl.ds(8 + near, NZ, stride=32)]
        for along, lane in enumerate((0, LY - 1)):
            column = jnp.sum(jnp.where(lane48 == lane, edge, 0.0), axis=1, keepdims=True)
            line = jnp.sum(jnp.where(eye48, column, 0.0), axis=0, keepdims=True)
            dgs[2 * side + along] = jnp.broadcast_to(line, (16, LY)).astype(BF16)

    xp_copy = [remote(xps.at[s], xpr.at[s], xp_ss.at[s], xp_rs.at[s], (gxs[s], gy)) for s in range(2)]
    dg_copy = [
        remote(dgs.at[n], dgr.at[n], dg_ss.at[n], dg_rs.at[n], (gxs[n // 2], gys[n % 2])) for n in range(4)
    ]
    for copy in xp_copy + dg_copy:
        copy.start()

    lane = lax.broadcasted_iota(jnp.int32, (CX, LY), 1)

    def pack_probe(block, _):
        packed = []
        for half in range(2):
            total = None
            for j in range(8):
                mine = pl.ds(pl.multiple_of((half * (NZ // 2) + block * 8 + j) * 32 + 8, 8), CX)
                face = PX[0, mine]
                for d in range(3):
                    speed = PX[1 + d, mine]
                    face = jnp.where(lane == 2 + d, pltpu.roll(speed, 2 + d, 1), face)
                    face = jnp.where(lane == 125 - d, pltpu.roll(speed, LY - 2 - d, 1), face)
                face = pltpu.roll(face, (16 * j + 8) % LY, 1)
                total = face if total is None else jnp.where((lane >> 4) == j, face, total)
            packed.append(total)
        rows = pl.ds(pl.multiple_of(block * CX, CX), CX)
        first = (lane & 15) < 8
        yps[0, rows] = jnp.where(first, pltpu.roll(packed[0], LY - 8, 1), packed[1]).astype(BF16)
        yps[1, rows] = jnp.where(first, packed[0], pltpu.roll(packed[1], 8, 1)).astype(BF16)

    loop(3, pack_probe, 1)
    yp_copy = [remote(yps.at[s], ypr.at[s], yp_ss.at[s], yp_rs.at[s], (gx, gys[s])) for s in range(2)]
    for copy in yp_copy:
        copy.start()
    def later_x(block, carry):
        pack_x(block)
        send_x(block)
        return carry

    lax.fori_loop(0, 3, later_x, 0)

    place = lane & 7
    layer = lane & 3

    def pack_y(i, _):
        packed = []
        for half in range(2):
            rows = pl.ds(pl.multiple_of(half * HALF + i * CX, CX), CX)
            v, p = VEL[1, rows], PR[rows]
            total = jnp.zeros((CX, LY), F32)
            for slot in range(NF):
                flux = fo[slot, rows]
                flux = (flux + p) * v if slot == 4 else flux * v
                flux = flux + p if slot == 2 else flux
                total = jnp.where((lane >> 3) == slot, pltpu.roll(flux, (4 + 8 * slot) % LY, 1), total)
            packed.append(total)
        rows = pl.ds(pl.multiple_of(i * CX, CX), CX)
        PY[0, rows] = jnp.where(place < 4, pltpu.roll(packed[0], LY - 4, 1), packed[1])
        PY[1, rows] = jnp.where(place < 4, packed[0], pltpu.roll(packed[1], 4, 1))

    loop(NZ // 2, pack_y, 3)
    deep = lax.broadcasted_iota(jnp.int32, (HALF // 4, LY), 1) & 3

    def shape_y(i, _):
        rows = pl.ds(pl.multiple_of(i * (HALF // 4), CX), HALF // 4)
        ys[0, rows] = shaped_lanes(PY[0, rows], deep, 1).astype(BF16)
        ys[1, rows] = shaped_lanes(PY[1, rows], 3 - deep, -1).astype(BF16)

    loop(4, shape_y, 1)
    y_copy = [remote(ys.at[s], yr.at[s], y_ss.at[s], y_rs.at[s], (gx, gys[s])) for s in range(2)]
    for copy in y_copy:
        copy.start()

    fill_weights(wd, wu)

    loads[3].wait()

    def chemistry(z, _):
        rows = pl.ds(pl.multiple_of(z * CX, CX), CX)
        moles = [fo[5 + k, rows] * (18.0 / MOLAR_MASS[k]) for k in range(9)]
        total = moles[0]
        for k in range(1, 9):
            total = total + moles[k]
        cold = (0.25 * total) / PR[rows]
        rates = [
            record[3] * jnp.exp(-record[4] * cold) * (moles[record[0]] * moles[record[1]]) for record in REACTIONS
        ]
        for k in range(NF):
            result = DECAY * ro[k, rows]
            for r in range(8):
                if TABLE[k, r] != 0.0:
                    result = result + float(STEP * TABLE[k, r]) * rates[r]
            ro[k, rows] = result

    loop(NZ, chemistry, 4)

    for s in range(2):
        xp_copy[s].wait_recv()
    for side, near, far in ((1, 7, 6), (0, 24, 25)):
        PX[0, pl.ds(near, NZ, stride=32)] = xpr[side, 0].astype(F32)
        PX[0, pl.ds(far, NZ, stride=32)] = xpr[side, 1].astype(F32)
        for d in range(3):
            PX[1 + d, pl.ds(near, NZ, stride=32)] = xpr[side, 2 + d].astype(F32)
    for n in range(4):
        dg_copy[n].wait_recv()
    for side, row in ((1, 7), (0, 24)):
        corner = []
        for along in (1, 0):
            line = dgr[2 * side + along].astype(F32)[0:1]
            corner.append(jnp.sum(jnp.where(eye48, line, 0.0), axis=1, keepdims=True))
        TX[pl.ds(row, NZ, stride=32)] = jnp.where(lane48 < 64, corner[0], corner[1])
    for s in range(2):
        yp_copy[s].wait_recv()

    def turned(block, _):
        there = pl.ds(pl.multiple_of(block * CX, CX), CX)
        low, high = ypr[1, there].astype(F32), ypr[0, there].astype(F32)
        put = lambda a, source, target: pltpu.roll(a, (target - source) % LY, 1)
        for half, j in [(half, j) for half in range(2) for j in range(8)]:
            z = half * (NZ // 2) + block * 8 + j
            rows = pl.ds(pl.multiple_of(z * CX, CX), CX)
            mine = pl.ds(pl.multiple_of(z * 32 + 8, 8), CX)
            base = 16 * j + 8 * half
            s = PX[0, mine]
            t = jnp.where(lane < 64, pltpu.roll(s, 2, 1), pltpu.roll(s, LY - 2, 1))
            t = jnp.where(lane < 2, put(low, base + 6, 0), t)
            TX[mine] = jnp.where(lane >= 126, put(high, base, 126), t)
            for d in range(3):
                YH[d, rows] = jnp.where(lane < 64, put(low, base + 5 - d, 0), put(high, base + 2 + d, 127))

    loop(3, turned, 1)

    def normals(z, turn):
        above, below = lax.rem(z + 1, NZ), lax.rem(z + NZ - 1, NZ)
        rows = pl.ds(pl.multiple_of(z * CX, CX), CX)

        def wide(ref, plane, shift):
            return ref[0, pl.ds(plane * 32 + 4 + shift, 24)]

        def mine(plane, shift=0):
            return pl.ds(plane * 32 + 8 + shift, CX)

        lane24 = lax.broadcasted_iota(jnp.int32, (24, LY), 1)
        s, t = wide(PX, z, 0), TX[pl.ds(z * 32 + 4, 24)]
        behind = jnp.where(lane24 == 0, pltpu.roll(t, LY - 1, 1), pltpu.roll(s, 1, 1))
        ahead = jnp.where(lane24 == LY - 1, pltpu.roll(t, 1, 1), pltpu.roll(s, LY - 1, 1))
        grad_x = 0.5 * (wide(PX, z, 1) - wide(PX, z, -1))
        grad_y = 0.5 * (ahead - behind)
        grad_z = 0.5 * (wide(PX, above, 0) - wide(PX, below, 0))
        scale = -lax.rsqrt(jnp.maximum(grad_x * grad_x + grad_y * grad_y + grad_z * grad_z, 0.01))
        NS[turn, 0], NS[turn, 1], NS[turn, 2] = grad_x * scale, grad_y * scale, grad_z * scale
        normal = [NS[turn, d, 4:20] for d in range(3)]

        t = TX[mine(z)]
        edge_x = 0.5 * (TX[mine(z, 1)] - TX[mine(z, -1)])
        edge_y = 0.5 * (pltpu.roll(t, LY - 1, 1) - pltpu.roll(t, 1, 1))
        edge_z = 0.5 * (TX[mine(above)] - TX[mine(below)])
        edge = -edge_y * lax.rsqrt(jnp.maximum(edge_x * edge_x + edge_y * edge_y + edge_z * edge_z, 0.01))
        behind = jnp.where(lane == 0, pltpu.roll(edge, LY - 1, 1), pltpu.roll(normal[1], 1, 1))
        ahead = jnp.where(lane == LY - 1, pltpu.roll(edge, 1, 1), pltpu.roll(normal[1], LY - 1, 1))
        CV[rows] = 0.5 * (NS[turn, 0, 5:21] - NS[turn, 0, 3:19]) + 0.5 * (ahead - behind)
        NZS[rows] = normal[2]

        strain = None
        for d in range(3):
            speed, halo = PX[1 + d, mine(z)], YH[d, rows]
            behind = jnp.where(lane == 0, halo, pltpu.roll(speed, 1, 1))
            ahead = jnp.where(lane == LY - 1, halo, pltpu.roll(speed, LY - 1, 1))
            along = (
                0.5 * (PX[1 + d, mine(z, 1)] - PX[1 + d, mine(z, -1)]),
                0.5 * (ahead - behind),
                0.5 * (PX[1 + d, mine(above)] - PX[1 + d, mine(below)]),
            )
            inner = normal[0] * along[0] + normal[1] * along[1] + normal[2] * along[2]
            term = along[d] - normal[d] * inner
            strain = term if strain is None else strain + term
        for d in range(3):
            M[d, z] = normal[d].astype(BF16)
        M[4, z] = strain.astype(BF16)

    loop(NZ, normals, 3)

    depth = NZ // 8

    def curve(z, _):
        above, below = lax.rem(z + 1, NZ), lax.rem(z + NZ - 1, NZ)
        at = lambda plane: pl.ds(pl.multiple_of(plane * CX, CX), CX)
        M[3, z] = (CV[at(z)] + 0.5 * (NZS[at(above)] - NZS[at(below)])).astype(BF16)

    loop(NZ, curve, 6)
    land = mo.at[:, :, :, pl.ds(pl.multiple_of(gy * LY, LY), LY)]

    def m_copy(d):
        target = lax.rem(gy + d, ny)
        return remote(M.at[:, pl.ds(target * depth, depth)], land, m_ss.at[d], m_rs.at[d], (gx, target))

    for d in range(1, 8):
        m_copy(d).start()
    own = pltpu.make_async_copy(M.at[:, pl.ds(gy * depth, depth)], land, own_sem)
    own.start()

    def pass_z(i, carry):
        first, tile = lax.div(i, 2) * 8, lax.rem(i, 2) * 8
        at = [
            pl.ds(pl.multiple_of(lax.rem(first + (j + NZ - 4), NZ) * CX + tile, 8), 8) for j in range(16)
        ]
        w = [VEL[2, a] for a in at]
        for k in range(NF):
            flux = [fo[k, a] for a in at]
            if k == 4:
                flux = [flux[j] + PR[at[j]] for j in range(16)]
            flux = [flux[j] * w[j] for j in range(16)]
            if k == 3:
                flux = [flux[j] + PR[at[j]] for j in range(16)]
            before = [ro[k, a] for a in at[4:12]]
            after = []
            for j in range(4, 12):
                change = (STEP * C[0]) * (flux[j - 1] - flux[j + 1])
                for m in range(2, 5):
                    change = change + (STEP * C[m - 1]) * (flux[j - m] - flux[j + m])
                after.append(before[j - 4] + change)
            for j in range(4, 12):
                ro[k, at[j]] = after[j - 4]
        return carry

    lax.fori_loop(0, NZ // 4, pass_z, 0)

    def layer_x(side, block, k, n, part):
        half = slice(8 * part, 8 * part + 8)
        if (k, n) in KNOWN:
            probe = xpr[side, KNOWN[k, n], pl.ds(pl.multiple_of(block * 16, 16), 16)].astype(F32)[half]
            return known_flux(k, layer_x(side, block, 0, n, part), probe)
        return xr[side, block, pl.ds(SENT.index((k, n)) * 16, 16)].astype(F32)[half]

    def pass_x(block, carry):
        for side in range(2):
            x_copy(side, block).wait_recv()
        for part in range(2):
            at = [pl.ds(block * 256 + part * 128 + r, 8, stride=CX) for r in range(CX)]
            u = [VEL[0, a] for a in at]
            for k in range(NF):
                flux = [fo[k, a] for a in at]
                if k == 4:
                    flux = [flux[r] + PR[at[r]] for r in range(CX)]
                flux = [flux[r] * u[r] for r in range(CX)]
                if k == 1:
                    flux = [flux[r] + PR[at[r]] for r in range(CX)]
                low, high = [[layer_x(side, block, k, n, part) for n in range(4)] for side in (1, 0)]
                flux = low[::-1] + flux + high
                before = [ro[k, a] for a in at]
                after = []
                for r in range(CX):
                    change = (STEP * C[0]) * (flux[r + 3] - flux[r + 5])
                    for m in range(2, 5):
                        change = change + (STEP * C[m - 1]) * (flux[r + 4 - m] - flux[r + 4 + m])
                    after.append(before[r] + change)
                for r in range(CX):
                    ro[k, at[r]] = after[r]
        return carry

    lax.fori_loop(0, 3, pass_x, 0)

    for s in range(2):
        y_copy[s].wait_recv()

    def pass_y(half, carry):
        rows = pl.ds(pl.multiple_of(half * HALF, HALF), HALF)
        edges = jnp.concatenate([yr[1], yr[0]], axis=1)
        for k in range(NF):
            value, v = fo[k, rows], VEL[1, rows]
            flux = (value + PR[rows]) * v if k == 4 else value * v
            flux = flux + PR[rows] if k == 2 else flux
            high = flux.astype(BF16)
            rest = (flux - high.astype(F32)).astype(BF16)
            slope = jnp.dot(jnp.concatenate([high, rest], axis=1), wd[...], preferred_element_type=F32)
            slope = slope + jnp.dot(edges, wu[2 * k + half], preferred_element_type=F32)
            result = ro[k, rows] - (STEP / 840.0) * slope
            ro[k, rows] = result
        return carry

    lax.fori_loop(0, 2, pass_y, 0)

    for copy in xp_copy + dg_copy + yp_copy + y_copy:
        copy.wait_send()
    for side in range(2):
        for block in range(3):
            x_copy(side, block).wait_send()
    own.wait()
    for d in range(1, 8):
        m_copy(d).wait()


def place_out(f_in, r_in, m_in, f_out, r_out, m_out, new, sem):
    copies = [
        pltpu.make_async_copy(m_in, m_out, sem.at[0]),
        pltpu.make_async_copy(r_in.at[pl.ds(0, 7)], r_out.at[pl.ds(0, 7)], sem.at[1]),
        pltpu.make_async_copy(r_in.at[pl.ds(7, 7)], r_out.at[pl.ds(7, 7)], sem.at[2]),
    ]
    for copy in copies:
        copy.start()
    for part in range(7):
        for k in (2 * part, 2 * part + 1):

            def update(i, _, k=k):
                rows = pl.ds(pl.multiple_of(i * 192, 192), 192)
                new[k, rows] = f_in[k, rows] + WEIGHT * r_in[k, rows]

            loop(4, update, 1)
        at = pl.ds(2 * part, 2)
        copies.append(pltpu.make_async_copy(new.at[at], f_out.at[at], sem.at[3 + part]))
        copies[-1].start()
    for copy in copies:
        copy.wait()


def per_device(fields, register):
    flat = lambda a: a.reshape(NF, ROWS, LY)
    any_space, vmem = pl.BlockSpec(memory_space=pl.ANY), pl.BlockSpec(memory_space=pltpu.VMEM)
    hbm = pl.BlockSpec(memory_space=pltpu.HBM)
    dma = pltpu.SemaphoreType.DMA
    big = jax.ShapeDtypeStruct((NF, ROWS, LY), F32)
    fields_next, register_next, metrics = pl.pallas_call(
        kernel,
        out_shape=(
            pltpu.VMEM(big.shape, big.dtype),
            pltpu.VMEM(big.shape, big.dtype),
            pltpu.VMEM((5, 6, CX, 1024), BF16),
        ),
        in_specs=[hbm] * 2,
        out_specs=(vmem, vmem, vmem),
        scratch_shapes=[
            pltpu.VMEM((2 * LY, LY), BF16),
            pltpu.VMEM((2 * NF, 2 * LY, LY), BF16),
            pltpu.VMEM((3, ROWS, LY), F32),
            pltpu.VMEM((ROWS, LY), F32),
            pltpu.VMEM((4, NZ * 32, LY), F32),
            pltpu.VMEM((NZ * 32, LY), F32),
            pltpu.VMEM((3, ROWS, LY), F32),
            pltpu.VMEM((3, 3, 24, LY), F32),
            pltpu.VMEM((ROWS, LY), F32),
            pltpu.VMEM((ROWS, LY), F32),
            pltpu.VMEM((5, NZ, CX, LY), BF16),
            pltpu.VMEM((2, 5, NZ, LY), BF16),
            pltpu.VMEM((2, 5, NZ, LY), BF16),
            pltpu.VMEM((4, 16, LY), BF16),
            pltpu.VMEM((4, 16, LY), BF16),
            pltpu.VMEM((2, 48, LY), BF16),
            pltpu.VMEM((2, 48, LY), BF16),
            pltpu.VMEM((2, HALF, LY), F32),
            pltpu.VMEM((2, HALF, LY), BF16),
            pltpu.VMEM((2, HALF, LY), BF16),
            pltpu.VMEM((2, 3, len(SENT) * 16, LY), BF16),
            pltpu.VMEM((2, 3, len(SENT) * 16, LY), BF16),
            dma((4,)),
            dma((2,)),
            dma((2,)),
            dma((4,)),
            dma((4,)),
            dma((2,)),
            dma((2,)),
            dma((2,)),
            dma((2,)),
            dma((2, 3)),
            dma((2, 3)),
            dma((8,)),
            dma((8,)),
            dma(()),
        ],
        compiler_params=pltpu.CompilerParams(collective_id=0, has_side_effects=True, vmem_limit_bytes=40 << 20),
    )(flat(fields), flat(register))
    small = jax.ShapeDtypeStruct(metrics.shape, BF16)
    fields_next, register_next, metrics = pl.pallas_call(
        place_out,
        out_shape=(big, big, small),
        in_specs=[vmem] * 3,
        out_specs=(any_space,) * 3,
        scratch_shapes=[pltpu.VMEM(big.shape, F32), dma((10,))],
        compiler_params=pltpu.CompilerParams(vmem_limit_bytes=8 << 20),
    )(*(pltpu.with_memory_space_constraint(a, pltpu.VMEM) for a in (fields_next, register_next, metrics)))
    shape = fields.shape
    return fields_next.reshape(shape), register_next.reshape(shape), metrics


def solution(mesh):
    in_specs = (P(None, None, "gx", "gy"), P(None, None, "gx", "gy"))
    out_specs = (P(None, None, "gx", "gy"), P(None, None, "gx", "gy"), P(None, "gy", "gx", None))
    return jax.shard_map(per_device, mesh=mesh, in_specs=in_specs, out_specs=out_specs, check_vma=False)
```

```python
import jax
import jax.numpy as jnp
import numpy as np
from jax import lax
from jax.experimental import pallas as pl
from jax.experimental.pallas import tpu as pltpu
from jax.sharding import PartitionSpec as P

MESH = pl.DeviceIdType.MESH
F32, BF16 = jnp.float32, jnp.bfloat16
DECAY = -0.4178904745
STEP = 0.25
WEIGHT = 0.3792103129
C = (0.8, -0.2, 4.0 / 105.0, -1.0 / 280.0)
MOLAR_MASS = (2.0, 32.0, 16.0, 17.0, 18.0, 1.0, 33.0, 34.0, 28.0)
FORMATION_HEAT = (0.0, 0.0, 2.0, 0.3, -1.5, 3.0, 0.1, -0.4, 0.0)
REACTIONS = (
    (5, 1, (2, 3), 40.0, 2.0),
    (2, 0, (5, 3), 30.0, 1.2),
    (3, 0, (5, 4), 25.0, 0.8),
    (2, 4, (3, 3), 10.0, 1.6),
    (5, 1, (6,), 15.0, 0.2),
    (6, 5, (3, 3), 20.0, 0.3),
    (6, 6, (7, 1), 12.0, 0.4),
    (7, 8, (3, 3, 8), 8.0, 1.8),
)
NF, NZ, CX, LY = 14, 48, 16, 128
ROWS = NZ * CX
HALF = ROWS // 2


def make_table():
    table = np.zeros((14, 8))
    for column, record in enumerate(REACTIONS):
        change = np.zeros(9)
        change[record[0]] -= 1.0
        change[record[1]] -= 1.0
        for product in record[2]:
            change[product] += 1.0
        for species in range(9):
            mass_change = MOLAR_MASS[species] / 18.0 * change[species]
            table[5 + species, column] = mass_change
            table[4, column] -= FORMATION_HEAT[species] * mass_change
    return table


TABLE = make_table()


WHOLE = (672.0, -168.0, 32.0, -3.0)


def fill_weights(wd, wu):
    gap = lax.broadcasted_iota(jnp.int32, (LY, LY), 0) - lax.broadcasted_iota(jnp.int32, (LY, LY), 1)
    inner = jnp.zeros((LY, LY), F32)
    for m in range(1, 5):
        inner = jnp.where(gap == m, WHOLE[m - 1], jnp.where(gap == -m, -WHOLE[m - 1], inner))
    wd[0:LY] = inner.astype(BF16)
    wd[LY : 2 * LY] = inner.astype(BF16)

    def clear(i, carry):
        wu[i] = jnp.zeros((2 * LY, LY), BF16)
        return carry

    lax.fori_loop(0, 2 * NF, clear, 0)
    row, lane = lax.broadcasted_iota(jnp.int32, (16, LY), 0), lax.broadcasted_iota(jnp.int32, (16, LY), 1)
    tiles = []
    for offset in range(0, 16, 4):
        layer = row - offset
        low, high = jnp.zeros((16, LY), F32), jnp.zeros((16, LY), F32)
        for n in range(4):
            low = jnp.where(layer - lane == n, -WHOLE[3 - n], low)
            high = jnp.where(layer + (LY - 1) - lane == n, WHOLE[n], high)
        valid = (layer >= 0) & (layer < 4)
        tiles.append([jnp.where(valid, t, 0.0).astype(BF16) for t in (low, high)])
    for k in range(NF):
        for half in range(2):
            base = 8 * k + 4 * half
            first = base // 16 * 16
            wu[2 * k + half, first : first + 16] = tiles[base % 16 // 4][0]
            wu[2 * k + half, LY + first : LY + first + 16] = tiles[base % 16 // 4][1]


def rounded(x):
    return x.astype(BF16).astype(F32)


KNOWN = {(2, 0): 3, (3, 0): 4, (9, 0): 0, (9, 1): 1}
SENT = [(k, n) for k in range(NF) for n in range(4) if (k, n) not in KNOWN]


def known_flux(k, mass, probe):
    return mass * probe * 0.25 if k == 9 else mass * probe


def shaped(h, given=()):
    q1 = given[0] if len(given) > 0 else rounded(h[0])
    e1 = q1 - h[0]
    q2 = given[1] if len(given) > 1 else rounded(h[1] + 4.0 * e1)
    left = C[0] * e1 + C[1] * (q2 - h[1])
    q3 = rounded(h[2] - left * (1.0 / C[2]))
    left = left + C[2] * (q3 - h[2])
    return q1, q2, q3, h[3] - left * (1.0 / C[3])


def shaped_lanes(x, layer, turn):
    roll = lambda a, n: pltpu.roll(a, (turn * n) % LY, 1)
    q1 = rounded(x)
    e1 = jnp.where(layer == 0, q1 - x, 0.0)
    q2 = rounded(x + 4.0 * roll(e1, 1))
    e2 = jnp.where(layer == 1, q2 - x, 0.0)
    left = C[0] * roll(e1, 1) + C[1] * e2
    left = roll(left, 1)
    q3 = rounded(x - left * (1.0 / C[2]))
    left = roll(jnp.where(layer == 2, left + C[2] * (q3 - x), 0.0), 1)
    q4 = rounded(x - left * (1.0 / C[3]))
    return jnp.where(layer == 0, q1, jnp.where(layer == 1, q2, jnp.where(layer == 2, q3, q4)))


def loop(count, body, unroll):
    def several(i, carry):
        for j in range(unroll):
            body(i * unroll + j, j)
        return carry

    lax.fori_loop(0, count // unroll, several, 0)


def kernel(
    f_hbm, r_hbm, fo, ro, mo,
    wd, wu, VEL, PR, PX, TX, YH, NS, NZS, CV, M,
    xps, xpr, dgs, dgr, yps, ypr, PY, ys, yr, xs, xr,
    load_sem, xp_ss, xp_rs, dg_ss, dg_rs, yp_ss, yp_rs, y_ss, y_rs, x_ss, x_rs, m_ss, m_rs, own_sem,
):
    gx, gy = lax.axis_index("gx"), lax.axis_index("gy")
    nx, ny = lax.axis_size("gx"), lax.axis_size("gy")
    gxs = (lax.rem(gx + nx - 1, nx), lax.rem(gx + 1, nx))
    gys = (lax.rem(gy + ny - 1, ny), lax.rem(gy + 1, ny))

    barrier = pltpu.get_barrier_semaphore()
    partners = [(gxs[0], gy), (gxs[1], gy)]
    partners += [(gxs[a], gys[b]) for a in range(2) for b in range(2)]
    partners += [(gx, lax.rem(gy + d, ny)) for d in range(1, ny)]
    for partner in partners:
        pl.semaphore_signal(barrier, 1, device_id=partner, device_id_type=MESH)

    loads = [
        pltpu.make_async_copy(f_hbm.at[:, pl.ds(n * 256, 256)], fo.at[:, pl.ds(n * 256, 256)], load_sem.at[n])
        for n in range(3)
    ]
    loads.append(pltpu.make_async_copy(r_hbm, ro, load_sem.at[3]))
    for load in loads:
        load.start()

    def remote(src, dst, ss, rs, device):
        return pltpu.make_async_remote_copy(
            src_ref=src, dst_ref=dst, send_sem=ss, recv_sem=rs, device_id=device, device_id_type=MESH
        )

    def primitive(z, _):
        rows = pl.ds(pl.multiple_of(z * CX, CX), CX)
        mine = pl.ds(pl.multiple_of(z * 32 + 8, 8), CX)
        inverse = 1.0 / fo[0, rows]
        moment = [fo[1 + d, rows] for d in range(3)]
        speed = [m * inverse for m in moment]
        PR[rows] = 0.4 * (fo[4, rows] - 0.5 * (moment[0] * speed[0] + moment[1] * speed[1] + moment[2] * speed[2]))
        PX[0, mine] = rounded(4.0 * (fo[9, rows] * inverse))
        for d in range(3):
            VEL[d, rows] = speed[d]
            PX[1 + d, mine] = rounded(speed[d])

    def x_copy(side, block):
        return remote(
            xs.at[side, block], xr.at[side, block], x_ss.at[side, block], x_rs.at[side, block], (gxs[side], gy)
        )

    def pack_x(block):
        for side in range(2):
            at = [pl.ds(block * 256 + (n if side == 0 else 15 - n), 16, stride=CX) for n in range(4)]
            u = [VEL[0, a] for a in at]
            for k in range(NF):
                h = []
                for n in range(4):
                    flux = fo[k, at[n]]
                    flux = (flux + PR[at[n]]) * u[n] if k == 4 else flux * u[n]
                    h.append(flux + PR[at[n]] if k == 1 else flux)
                given = []
                for n in range(2):
                    if (k, n) in KNOWN:
                        row = n if side == 0 else 15 - n
                        probe = PX[{2: 2, 3: 3, 9: 0}[k], pl.ds(block * 512 + 8 + row, 16, stride=32)]
                        given.append(known_flux(k, mass[n], probe))
                q = shaped(h, given)
                mass = q[:2] if k == 0 else mass
                for n in range(4):
                    if (k, n) not in KNOWN:
                        xs[side, block, pl.ds(SENT.index((k, n)) * 16, 16)] = q[n].astype(BF16)

    def send_x(block):
        for side in range(2):
            x_copy(side, block).start()

    loads[0].wait()
    loop(16, primitive, 4)
    pl.semaphore_wait(barrier, len(partners))
    loads[1].wait()
    loads[2].wait()
    loop(32, lambda z, _: primitive(z + 16, _), 4)

    lane48 = lax.broadcasted_iota(jnp.int32, (NZ, LY), 1)
    eye48 = lane48 == lax.broadcasted_iota(jnp.int32, (NZ, LY), 0)
    for side, (near, far) in enumerate(((0, 1), (15, 14))):
        xps[side, 0] = PX[0, pl.ds(8 + near, NZ, stride=32)].astype(BF16)
        xps[side, 1] = PX[0, pl.ds(8 + far, NZ, stride=32)].astype(BF16)
        for d in range(3):
            xps[side, 2 + d] = PX[1 + d, pl.ds(8 + near, NZ, stride=32)].astype(BF16)
        edge = PX[0, pl.ds(8 + near, NZ, stride=32)]
        for along, lane in enumerate((0, LY - 1)):
            column = jnp.sum(jnp.where(lane48 == lane, edge, 0.0), axis=1, keepdims=True)
            line = jnp.sum(jnp.where(eye48, column, 0.0), axis=0, keepdims=True)
            dgs[2 * side + along] = jnp.broadcast_to(line, (16, LY)).astype(BF16)

    xp_copy = [remote(xps.at[s], xpr.at[s], xp_ss.at[s], xp_rs.at[s], (gxs[s], gy)) for s in range(2)]
    dg_copy = [
        remote(dgs.at[n], dgr.at[n], dg_ss.at[n], dg_rs.at[n], (gxs[n // 2], gys[n % 2])) for n in range(4)
    ]
    for copy in xp_copy + dg_copy:
        copy.start()

    lane = lax.broadcasted_iota(jnp.int32, (CX, LY), 1)

    def pack_probe(block, _):
        packed = []
        for half in range(2):
            total = None
            for j in range(8):
                mine = pl.ds(pl.multiple_of((half * (NZ // 2) + block * 8 + j) * 32 + 8, 8), CX)
                face = PX[0, mine]
                for d in range(3):
                    speed = PX[1 + d, mine]
                    face = jnp.where(lane == 2 + d, pltpu.roll(speed, 2 + d, 1), face)
                    face = jnp.where(lane == 125 - d, pltpu.roll(speed, LY - 2 - d, 1), face)
                face = pltpu.roll(face, (16 * j + 8) % LY, 1)
                total = face if total is None else jnp.where((lane >> 4) == j, face, total)
            packed.append(total)
        rows = pl.ds(pl.multiple_of(block * CX, CX), CX)
        first = (lane & 15) < 8
        yps[0, rows] = jnp.where(first, pltpu.roll(packed[0], LY - 8, 1), packed[1]).astype(BF16)
        yps[1, rows] = jnp.where(first, packed[0], pltpu.roll(packed[1], 8, 1)).astype(BF16)

    loop(3, pack_probe, 1)
    yp_copy = [remote(yps.at[s], ypr.at[s], yp_ss.at[s], yp_rs.at[s], (gx, gys[s])) for s in range(2)]
    for copy in yp_copy:
        copy.start()
    def later_x(block, carry):
        pack_x(block)
        send_x(block)
        return carry

    lax.fori_loop(0, 3, later_x, 0)

    fill_weights(wd, wu)

    loads[3].wait()

    def chemistry(z, _):
        rows = pl.ds(pl.multiple_of(z * CX, CX), CX)
        moles = [fo[5 + k, rows] * (18.0 / MOLAR_MASS[k]) for k in range(9)]
        total = moles[0]
        for k in range(1, 9):
            total = total + moles[k]
        cold = (0.25 * total) / PR[rows]
        rates = [
            record[3] * jnp.exp(-record[4] * cold) * (moles[record[0]] * moles[record[1]]) for record in REACTIONS
        ]
        for k in range(NF):
            result = DECAY * ro[k, rows]
            for r in range(8):
                if TABLE[k, r] != 0.0:
                    result = result + float(STEP * TABLE[k, r]) * rates[r]
            ro[k, rows] = result

    loop(NZ, chemistry, 4)

    place = lane & 7
    layer = lane & 3

    def pack_y(i, _):
        packed = []
        for half in range(2):
            rows = pl.ds(pl.multiple_of(half * HALF + i * CX, CX), CX)
            v, p = VEL[1, rows], PR[rows]
            total = jnp.zeros((CX, LY), F32)
            for slot in range(NF):
                flux = fo[slot, rows]
                flux = (flux + p) * v if slot == 4 else flux * v
                flux = flux + p if slot == 2 else flux
                total = jnp.where((lane >> 3) == slot, pltpu.roll(flux, (4 + 8 * slot) % LY, 1), total)
            packed.append(total)
        rows = pl.ds(pl.multiple_of(i * CX, CX), CX)
        PY[0, rows] = jnp.where(place < 4, pltpu.roll(packed[0], LY - 4, 1), packed[1])
        PY[1, rows] = jnp.where(place < 4, packed[0], pltpu.roll(packed[1], 4, 1))

    loop(NZ // 2, pack_y, 3)
    deep = lax.broadcasted_iota(jnp.int32, (HALF // 4, LY), 1) & 3

    def shape_y(i, _):
        rows = pl.ds(pl.multiple_of(i * (HALF // 4), CX), HALF // 4)
        ys[0, rows] = shaped_lanes(PY[0, rows], deep, 1).astype(BF16)
        ys[1, rows] = shaped_lanes(PY[1, rows], 3 - deep, -1).astype(BF16)

    loop(4, shape_y, 1)
    y_copy = [remote(ys.at[s], yr.at[s], y_ss.at[s], y_rs.at[s], (gx, gys[s])) for s in range(2)]
    for copy in y_copy:
        copy.start()

    for s in range(2):
        xp_copy[s].wait_recv()
    for side, near, far in ((1, 7, 6), (0, 24, 25)):
        PX[0, pl.ds(near, NZ, stride=32)] = xpr[side, 0].astype(F32)
        PX[0, pl.ds(far, NZ, stride=32)] = xpr[side, 1].astype(F32)
        for d in range(3):
            PX[1 + d, pl.ds(near, NZ, stride=32)] = xpr[side, 2 + d].astype(F32)
    for n in range(4):
        dg_copy[n].wait_recv()
    for side, row in ((1, 7), (0, 24)):
        corner = []
        for along in (1, 0):
            line = dgr[2 * side + along].astype(F32)[0:1]
            corner.append(jnp.sum(jnp.where(eye48, line, 0.0), axis=1, keepdims=True))
        TX[pl.ds(row, NZ, stride=32)] = jnp.where(lane48 < 64, corner[0], corner[1])
    for s in range(2):
        yp_copy[s].wait_recv()

    def turned(block, _):
        there = pl.ds(pl.multiple_of(block * CX, CX), CX)
        low, high = ypr[1, there].astype(F32), ypr[0, there].astype(F32)
        put = lambda a, source, target: pltpu.roll(a, (target - source) % LY, 1)
        for half, j in [(half, j) for half in range(2) for j in range(8)]:
            z = half * (NZ // 2) + block * 8 + j
            rows = pl.ds(pl.multiple_of(z * CX, CX), CX)
            mine = pl.ds(pl.multiple_of(z * 32 + 8, 8), CX)
            base = 16 * j + 8 * half
            s = PX[0, mine]
            t = jnp.where(lane < 64, pltpu.roll(s, 2, 1), pltpu.roll(s, LY - 2, 1))
            t = jnp.where(lane < 2, put(low, base + 6, 0), t)
            TX[mine] = jnp.where(lane >= 126, put(high, base, 126), t)
            for d in range(3):
                YH[d, rows] = jnp.where(lane < 64, put(low, base + 5 - d, 0), put(high, base + 2 + d, 127))

    loop(3, turned, 1)

    def normals(z, turn):
        above, below = lax.rem(z + 1, NZ), lax.rem(z + NZ - 1, NZ)
        rows = pl.ds(pl.multiple_of(z * CX, CX), CX)

        def wide(ref, plane, shift):
            return ref[0, pl.ds(plane * 32 + 4 + shift, 24)]

        def mine(plane, shift=0):
            return pl.ds(plane * 32 + 8 + shift, CX)

        lane24 = lax.broadcasted_iota(jnp.int32, (24, LY), 1)
        s, t = wide(PX, z, 0), TX[pl.ds(z * 32 + 4, 24)]
        behind = jnp.where(lane24 == 0, pltpu.roll(t, LY - 1, 1), pltpu.roll(s, 1, 1))
        ahead = jnp.where(lane24 == LY - 1, pltpu.roll(t, 1, 1), pltpu.roll(s, LY - 1, 1))
        grad_x = 0.5 * (wide(PX, z, 1) - wide(PX, z, -1))
        grad_y = 0.5 * (ahead - behind)
        grad_z = 0.5 * (wide(PX, above, 0) - wide(PX, below, 0))
        scale = -lax.rsqrt(jnp.maximum(grad_x * grad_x + grad_y * grad_y + grad_z * grad_z, 0.01))
        NS[turn, 0], NS[turn, 1], NS[turn, 2] = grad_x * scale, grad_y * scale, grad_z * scale
        normal = [NS[turn, d, 4:20] for d in range(3)]

        t = TX[mine(z)]
        edge_x = 0.5 * (TX[mine(z, 1)] - TX[mine(z, -1)])
        edge_y = 0.5 * (pltpu.roll(t, LY - 1, 1) - pltpu.roll(t, 1, 1))
        edge_z = 0.5 * (TX[mine(above)] - TX[mine(below)])
        edge = -edge_y * lax.rsqrt(jnp.maximum(edge_x * edge_x + edge_y * edge_y + edge_z * edge_z, 0.01))
        behind = jnp.where(lane == 0, pltpu.roll(edge, LY - 1, 1), pltpu.roll(normal[1], 1, 1))
        ahead = jnp.where(lane == LY - 1, pltpu.roll(edge, 1, 1), pltpu.roll(normal[1], LY - 1, 1))
        CV[rows] = 0.5 * (NS[turn, 0, 5:21] - NS[turn, 0, 3:19]) + 0.5 * (ahead - behind)
        NZS[rows] = normal[2]

        strain = None
        for d in range(3):
            speed, halo = PX[1 + d, mine(z)], YH[d, rows]
            behind = jnp.where(lane == 0, halo, pltpu.roll(speed, 1, 1))
            ahead = jnp.where(lane == LY - 1, halo, pltpu.roll(speed, LY - 1, 1))
            along = (
                0.5 * (PX[1 + d, mine(z, 1)] - PX[1 + d, mine(z, -1)]),
                0.5 * (ahead - behind),
                0.5 * (PX[1 + d, mine(above)] - PX[1 + d, mine(below)]),
            )
            inner = normal[0] * along[0] + normal[1] * along[1] + normal[2] * along[2]
            term = along[d] - normal[d] * inner
            strain = term if strain is None else strain + term
        for d in range(3):
            M[d, z] = normal[d].astype(BF16)
        M[4, z] = strain.astype(BF16)

    loop(NZ, normals, 3)

    depth = NZ // 8

    def curve(z, _):
        above, below = lax.rem(z + 1, NZ), lax.rem(z + NZ - 1, NZ)
        at = lambda plane: pl.ds(pl.multiple_of(plane * CX, CX), CX)
        M[3, z] = (CV[at(z)] + 0.5 * (NZS[at(above)] - NZS[at(below)])).astype(BF16)

    loop(NZ, curve, 6)
    land = mo.at[:, :, :, pl.ds(pl.multiple_of(gy * LY, LY), LY)]

    def m_copy(d):
        target = lax.rem(gy + d, ny)
        return remote(M.at[:, pl.ds(target * depth, depth)], land, m_ss.at[d], m_rs.at[d], (gx, target))

    for d in range(1, 8):
        m_copy(d).start()
    own = pltpu.make_async_copy(M.at[:, pl.ds(gy * depth, depth)], land, own_sem)
    own.start()

    def pass_z(i, carry):
        first, tile = lax.div(i, 2) * 8, lax.rem(i, 2) * 8
        at = [
            pl.ds(pl.multiple_of(lax.rem(first + (j + NZ - 4), NZ) * CX + tile, 8), 8) for j in range(16)
        ]
        w = [VEL[2, a] for a in at]
        for k in range(NF):
            flux = [fo[k, a] for a in at]
            if k == 4:
                flux = [flux[j] + PR[at[j]] for j in range(16)]
            flux = [flux[j] * w[j] for j in range(16)]
            if k == 3:
                flux = [flux[j] + PR[at[j]] for j in range(16)]
            before = [ro[k, a] for a in at[4:12]]
            after = []
            for j in range(4, 12):
                change = (STEP * C[0]) * (flux[j - 1] - flux[j + 1])
                for m in range(2, 5):
                    change = change + (STEP * C[m - 1]) * (flux[j - m] - flux[j + m])
                after.append(before[j - 4] + change)
            for j in range(4, 12):
                ro[k, at[j]] = after[j - 4]
        return carry

    lax.fori_loop(0, NZ // 4, pass_z, 0)

    def layer_x(side, block, k, n, part):
        half = slice(8 * part, 8 * part + 8)
        if (k, n) in KNOWN:
            probe = xpr[side, KNOWN[k, n], pl.ds(pl.multiple_of(block * 16, 16), 16)].astype(F32)[half]
            return known_flux(k, layer_x(side, block, 0, n, part), probe)
        return xr[side, block, pl.ds(SENT.index((k, n)) * 16, 16)].astype(F32)[half]

    def pass_x(block, carry):
        for side in range(2):
            x_copy(side, block).wait_recv()
        for part in range(2):
            at = [pl.ds(block * 256 + part * 128 + r, 8, stride=CX) for r in range(CX)]
            u = [VEL[0, a] for a in at]
            for k in range(NF):
                flux = [fo[k, a] for a in at]
                if k == 4:
                    flux = [flux[r] + PR[at[r]] for r in range(CX)]
                flux = [flux[r] * u[r] for r in range(CX)]
                if k == 1:
                    flux = [flux[r] + PR[at[r]] for r in range(CX)]
                low, high = [[layer_x(side, block, k, n, part) for n in range(4)] for side in (1, 0)]
                flux = low[::-1] + flux + high
                before = [ro[k, a] for a in at]
                after = []
                for r in range(CX):
                    change = (STEP * C[0]) * (flux[r + 3] - flux[r + 5])
                    for m in range(2, 5):
                        change = change + (STEP * C[m - 1]) * (flux[r + 4 - m] - flux[r + 4 + m])
                    after.append(before[r] + change)
                for r in range(CX):
                    ro[k, at[r]] = after[r]
        return carry

    lax.fori_loop(0, 3, pass_x, 0)

    for s in range(2):
        y_copy[s].wait_recv()

    def pass_y(half, carry):
        rows = pl.ds(pl.multiple_of(half * HALF, HALF), HALF)
        edges = jnp.concatenate([yr[1], yr[0]], axis=1)
        for k in range(NF):
            value, v = fo[k, rows], VEL[1, rows]
            flux = (value + PR[rows]) * v if k == 4 else value * v
            flux = flux + PR[rows] if k == 2 else flux
            high = flux.astype(BF16)
            rest = (flux - high.astype(F32)).astype(BF16)
            slope = jnp.dot(jnp.concatenate([high, rest], axis=1), wd[...], preferred_element_type=F32)
            slope = slope + jnp.dot(edges, wu[2 * k + half], preferred_element_type=F32)
            result = ro[k, rows] - (STEP / 840.0) * slope
            ro[k, rows] = result
        return carry

    lax.fori_loop(0, 2, pass_y, 0)

    for copy in xp_copy + dg_copy + yp_copy + y_copy:
        copy.wait_send()
    for side in range(2):
        for block in range(3):
            x_copy(side, block).wait_send()
    own.wait()
    for d in range(1, 8):
        m_copy(d).wait()


def place_out(f_in, r_in, m_in, f_out, r_out, m_out, new, sem):
    copies = [
        pltpu.make_async_copy(m_in, m_out, sem.at[0]),
        pltpu.make_async_copy(r_in.at[pl.ds(0, 7)], r_out.at[pl.ds(0, 7)], sem.at[1]),
        pltpu.make_async_copy(r_in.at[pl.ds(7, 7)], r_out.at[pl.ds(7, 7)], sem.at[2]),
    ]
    for copy in copies:
        copy.start()
    for part in range(7):
        for k in (2 * part, 2 * part + 1):

            def update(i, _, k=k):
                rows = pl.ds(pl.multiple_of(i * 192, 192), 192)
                new[k, rows] = f_in[k, rows] + WEIGHT * r_in[k, rows]

            loop(4, update, 1)
        at = pl.ds(2 * part, 2)
        copies.append(pltpu.make_async_copy(new.at[at], f_out.at[at], sem.at[3 + part]))
        copies[-1].start()
    for copy in copies:
        copy.wait()


def per_device(fields, register):
    flat = lambda a: a.reshape(NF, ROWS, LY)
    any_space, vmem = pl.BlockSpec(memory_space=pl.ANY), pl.BlockSpec(memory_space=pltpu.VMEM)
    hbm = pl.BlockSpec(memory_space=pltpu.HBM)
    dma = pltpu.SemaphoreType.DMA
    big = jax.ShapeDtypeStruct((NF, ROWS, LY), F32)
    fields_next, register_next, metrics = pl.pallas_call(
        kernel,
        out_shape=(
            pltpu.VMEM(big.shape, big.dtype),
            pltpu.VMEM(big.shape, big.dtype),
            pltpu.VMEM((5, 6, CX, 1024), BF16),
        ),
        in_specs=[hbm] * 2,
        out_specs=(vmem, vmem, vmem),
        scratch_shapes=[
            pltpu.VMEM((2 * LY, LY), BF16),
            pltpu.VMEM((2 * NF, 2 * LY, LY), BF16),
            pltpu.VMEM((3, ROWS, LY), F32),
            pltpu.VMEM((ROWS, LY), F32),
            pltpu.VMEM((4, NZ * 32, LY), F32),
            pltpu.VMEM((NZ * 32, LY), F32),
            pltpu.VMEM((3, ROWS, LY), F32),
            pltpu.VMEM((3, 3, 24, LY), F32),
            pltpu.VMEM((ROWS, LY), F32),
            pltpu.VMEM((ROWS, LY), F32),
            pltpu.VMEM((5, NZ, CX, LY), BF16),
            pltpu.VMEM((2, 5, NZ, LY), BF16),
            pltpu.VMEM((2, 5, NZ, LY), BF16),
            pltpu.VMEM((4, 16, LY), BF16),
            pltpu.VMEM((4, 16, LY), BF16),
            pltpu.VMEM((2, 48, LY), BF16),
            pltpu.VMEM((2, 48, LY), BF16),
            pltpu.VMEM((2, HALF, LY), F32),
            pltpu.VMEM((2, HALF, LY), BF16),
            pltpu.VMEM((2, HALF, LY), BF16),
            pltpu.VMEM((2, 3, len(SENT) * 16, LY), BF16),
            pltpu.VMEM((2, 3, len(SENT) * 16, LY), BF16),
            dma((4,)),
            dma((2,)),
            dma((2,)),
            dma((4,)),
            dma((4,)),
            dma((2,)),
            dma((2,)),
            dma((2,)),
            dma((2,)),
            dma((2, 3)),
            dma((2, 3)),
            dma((8,)),
            dma((8,)),
            dma(()),
        ],
        compiler_params=pltpu.CompilerParams(collective_id=0, has_side_effects=True, vmem_limit_bytes=40 << 20),
    )(flat(fields), flat(register))
    small = jax.ShapeDtypeStruct(metrics.shape, BF16)
    fields_next, register_next, metrics = pl.pallas_call(
        place_out,
        out_shape=(big, big, small),
        in_specs=[vmem] * 3,
        out_specs=(any_space,) * 3,
        scratch_shapes=[pltpu.VMEM(big.shape, F32), dma((10,))],
        compiler_params=pltpu.CompilerParams(vmem_limit_bytes=8 << 20),
    )(*(pltpu.with_memory_space_constraint(a, pltpu.VMEM) for a in (fields_next, register_next, metrics)))
    shape = fields.shape
    return fields_next.reshape(shape), register_next.reshape(shape), metrics


def solution(mesh):
    in_specs = (P(None, None, "gx", "gy"), P(None, None, "gx", "gy"))
    out_specs = (P(None, None, "gx", "gy"), P(None, None, "gx", "gy"), P(None, "gy", "gx", None))
    return jax.shard_map(per_device, mesh=mesh, in_specs=in_specs, out_specs=out_specs, check_vma=False)
```
